32 devices in a mesh: dp: 8 (over y, x, core), mp: 4 (over z).
Axes of the slice: x: 2, y: 2, z: 4, core: 2. Of those that a mesh axis runs over, the one named last changes fastest.
Arguments:
- grid_latent: bfloat16 [8, 1024, 1024], P('dp', 'mp'), may hold values from -6 to 6
- mesh_latent: bfloat16 [8, 512, 1024], P('dp', 'mp'), may hold values from -6 to 6
- edge_source: int32 [8, 3072], P('dp', 'mp'), may hold values from 0 to 1023, as said below
- edge_dest: int32 [8, 3072], P('dp', 'mp'), may hold values from 0 to 511, as said below
- edge_count: int32 [8, 4], P('dp', 'mp'), may hold values from 256 to 768, as said below
- edge_attr: float32 [8, 4, 3072], P('dp', None, 'mp'), may hold values from -5 to 5
- w_attr: float32 [4, 1024], replicated, may hold values from -3 to 3
- w_in: bfloat16 [1024, 1024], replicated, may hold values from -0.1875 to 0.1875
- w_out: bfloat16 [1024, 1024], replicated, may hold values from -0.1875 to 0.1875
- w_qkv: bfloat16 [3, 1024, 1024], P(None, None, 'mp')
- w_o: bfloat16 [1024, 1024], P('mp'), may hold values from -0.1875 to 0.1875
- cotangent: bfloat16 [8, 512, 1024], P('dp', 'mp'), may hold values from -6 to 6
Outputs:
- d_grid: bfloat16 [8, 1024, 1024], P('dp', 'mp')
- d_mesh: bfloat16 [8, 512, 1024], P('dp', 'mp')
- d_w_attr: float32 [4, 1024], replicated
- d_w_in: float32 [1024, 1024], P('dp', 'mp')
- d_w_out: float32 [1024, 1024], P('dp', 'mp')
- d_w_qkv: float32 [3, 1024, 1024], P(None, 'dp', 'mp')
- d_w_o: float32 [1024, 1024], P('mp', 'dp')
The draws below stay inside these ranges and needn't reach their ends.
Inputs may be any that keep to these rules, and one draw needn't show every extreme that they name: `edge_source`: edge slots of band b (positions b * 768 to (b + 1) * 768 - 1 of a sample) name grid points of band b, rows b * 256 to (b + 1) * 256 - 1. `edge_dest`: edge slots of band b name mesh nodes of band b - 1, b or b + 1 (bands of 128 nodes each). `edge_count`: the first and last bands of every sample are full.
All inputs are finite; a program needn't handle non-finite values.
Results may differ from the reference program's by a relative error of at most 0.025.
Values may be sent and summed in bfloat16 or wider, within the bound.
A program may use at most 128 MiB of HBM per device.

```python
import jax
import jax.numpy as jnp
from jax import lax

C = 1024
HEADS = 16
HDIM = 64
ATTR = 4
GRID_DEV = 256
EDGES_DEV = 768
NODE_DEV = 128
SAMPLES = 8
GRID = 1024
EDGES = 3072
MESH = 512


def draw_edge_source(key, part):
    band = jnp.arange(EDGES, dtype=jnp.int32) // EDGES_DEV
    local = jax.random.randint(jax.random.fold_in(key, 11), (SAMPLES, EDGES), 0, GRID_DEV)
    return (band[None, :] * GRID_DEV + local).astype(jnp.int32)


def draw_edge_dest(key, part):
    bands = EDGES // EDGES_DEV
    band = jnp.arange(EDGES, dtype=jnp.int32) // EDGES_DEV
    first = jax.random.fold_in(key, 23)
    second = jax.random.fold_in(key, 29)
    offset = jax.random.randint(first, (SAMPLES, EDGES), -1, 2)
    target = jnp.clip(band[None, :] + offset, 0, bands - 1)
    local = jax.random.randint(second, (SAMPLES, EDGES), 0, NODE_DEV)
    return (target * NODE_DEV + local).astype(jnp.int32)


def draw_edge_count(key, part):
    bands = EDGES // EDGES_DEV
    counts = jax.random.randint(jax.random.fold_in(key, 31), (SAMPLES, bands), EDGES_DEV // 3, EDGES_DEV + 1)
    counts = counts.at[:, 0].set(EDGES_DEV)
    counts = counts.at[:, bands - 1].set(EDGES_DEV)
    return counts.astype(jnp.int32)


def draw_w_qkv(key, part):
    base = jax.random.normal(jax.random.fold_in(key, 37), (3, C, C), jnp.float32) / jnp.sqrt(jnp.float32(C))
    return base.astype(jnp.bfloat16)


def level_of(stream_key, shape, pieces, low, top_value):
    loudness, own = 1.0, jax.random.fold_in(stream_key, 6)
    for dim, shards_of in pieces:
        draws = jnp.exp(jax.random.uniform(jax.random.fold_in(own, dim), (shards_of,), jnp.float32, low / len(pieces), top_value / len(pieces)))
        loudness = loudness * jnp.repeat(draws, shape[dim] // shards_of).reshape([-1 if axis == dim else 1 for axis in range(len(shape))])
    return loudness


def bell_draw(stream_key, extent, spread, reach, pieces=(), kind=jnp.bfloat16):
    values = jax.random.normal(stream_key, extent, jnp.float32) * spread
    if len(pieces) > 0:
        values = level_of(stream_key, extent, pieces, -0.22, 0.18) * values
    return jnp.clip(values, min=-reach, max=reach).astype(kind)


def setup_inputs(seed: int = 0) -> dict:
    streams_of = jax.random.split(jax.random.key(seed), 13)
    grid_latent = bell_draw(streams_of[0], (SAMPLES, GRID, C), 1.0, 6.0, ((0, 8), (1, 4)))
    mesh_latent = bell_draw(streams_of[1], (SAMPLES, MESH, C), 1.0, 6.0, ((0, 8), (1, 4)))
    edge_source = draw_edge_source(jax.random.fold_in(streams_of[12], 71), 0)
    edge_dest = draw_edge_dest(jax.random.fold_in(streams_of[12], 71), 0)
    edge_count = draw_edge_count(jax.random.fold_in(streams_of[12], 71), 0)
    edge_attr = bell_draw(streams_of[5], (SAMPLES, ATTR, EDGES), 1.0, 5.0, ((0, 8), (2, 4)), jnp.float32)
    w_attr = bell_draw(streams_of[6], (ATTR, C), ATTR ** -0.5, 3.0, (), jnp.float32)
    w_in = bell_draw(streams_of[7], (C, C), C ** -0.5, 0.1875)
    w_out = bell_draw(streams_of[8], (C, C), C ** -0.5, 0.1875)
    w_qkv = draw_w_qkv(jax.random.fold_in(streams_of[12], 71), 0)
    w_o = bell_draw(streams_of[10], (C, C), C ** -0.5, 0.1875, ((0, 4),))
    cotangent = bell_draw(streams_of[11], (SAMPLES, MESH, C), 1.0, 6.0, ((0, 8), (1, 4)))
    return {"grid_latent": grid_latent, "mesh_latent": mesh_latent, "edge_source": edge_source, "edge_dest": edge_dest, "edge_count": edge_count, "edge_attr": edge_attr, "w_attr": w_attr, "w_in": w_in, "w_out": w_out, "w_qkv": w_qkv, "w_o": w_o, "cotangent": cotangent}


EPS = 1e-06

def attend_head(q, k, v, d_att):
    scale = HDIM ** (-0.5)
    scores = jnp.dot(q, k.T, preferred_element_type=jnp.float32) * scale
    probs = jax.nn.softmax(scores, axis=-1)
    probs_b = probs.astype(jnp.bfloat16)
    attended = jnp.dot(probs_b, v, preferred_element_type=jnp.float32).astype(jnp.bfloat16)
    dprob = jnp.dot(d_att, v.T, preferred_element_type=jnp.float32)
    delta = lax.optimization_barrier(jnp.sum(probs * dprob, axis=-1, keepdims=True))
    dscore = (probs * (dprob - delta) * scale).astype(jnp.bfloat16)
    dq = jnp.dot(dscore, k, preferred_element_type=jnp.float32).astype(jnp.bfloat16)
    dk = jnp.dot(dscore.T, q, preferred_element_type=jnp.float32).astype(jnp.bfloat16)
    dv = jnp.dot(probs_b.T, d_att, preferred_element_type=jnp.float32).astype(jnp.bfloat16)
    return (attended, dq, dk, dv)

def one_sample(grid, mesh, source, dest, count, attr, cot, w_attr, w_in, w_out, w_qkv, w_o):
    position = jnp.arange(EDGES, dtype=jnp.int32)
    limit = jnp.take(count, position // EDGES_DEV)
    live = (position % EDGES_DEV < limit).astype(jnp.float32)[:, None]
    projected = jnp.dot(grid, w_in, preferred_element_type=jnp.float32)
    attr_terms = jnp.dot(attr.T, w_attr, precision=lax.Precision.HIGHEST, preferred_element_type=jnp.float32)
    preact = projected[source] + attr_terms
    hidden = (jax.nn.silu(preact) * live).astype(jnp.bfloat16)
    message = jnp.dot(hidden, w_out, preferred_element_type=jnp.float32).astype(jnp.bfloat16)
    gathered = jax.ops.segment_sum(message.astype(jnp.float32), dest, num_segments=MESH)
    node = mesh.astype(jnp.float32) + gathered
    inv = lax.rsqrt(lax.optimization_barrier(jnp.mean(node * node, axis=-1, keepdims=True)) + EPS)
    normed = (node * inv).astype(jnp.bfloat16)
    qkv = jnp.stack([jnp.dot(normed, w_qkv[i], preferred_element_type=jnp.float32) for i in range(3)]).astype(jnp.bfloat16)
    heads = qkv.reshape(3, MESH, HEADS, HDIM).transpose(0, 2, 1, 3)
    d_att = jnp.dot(cot, w_o.T, preferred_element_type=jnp.float32).astype(jnp.bfloat16)
    d_att = d_att.reshape(MESH, HEADS, HDIM).transpose(1, 0, 2)
    attended, dq, dk, dv = lax.map(lambda t: attend_head(t[0], t[1], t[2], t[3]), (heads[0], heads[1], heads[2], d_att))

    def joined(a):
        return a.transpose(1, 0, 2).reshape(MESH, C)
    attended = joined(attended)
    dqkv = jnp.stack([joined(dq), joined(dk), joined(dv)])
    dw_o = jnp.dot(attended.T, cot, preferred_element_type=jnp.float32)
    dw_qkv = jnp.einsum('nc,ind->icd', normed.astype(jnp.float32), dqkv.astype(jnp.float32))
    dx = jnp.dot(dqkv[0], w_qkv[0].T, preferred_element_type=jnp.float32)
    dx = dx + jnp.dot(dqkv[1], w_qkv[1].T, preferred_element_type=jnp.float32)
    dx = dx + jnp.dot(dqkv[2], w_qkv[2].T, preferred_element_type=jnp.float32)
    dnode = cot.astype(jnp.float32) + inv * dx - node * inv * inv * inv * lax.optimization_barrier(jnp.mean(dx * node, axis=-1, keepdims=True))
    d_mesh = dnode.astype(jnp.bfloat16)
    dmessage = (d_mesh[dest].astype(jnp.float32) * live).astype(jnp.bfloat16)
    dw_out = jnp.dot(hidden.T, dmessage, preferred_element_type=jnp.float32)
    dhidden = jnp.dot(dmessage, w_out.T, preferred_element_type=jnp.float32)
    sigma = jax.nn.sigmoid(preact)
    dpre = dhidden * sigma * (1.0 + preact * (1.0 - sigma)) * live
    dw_attr = jnp.dot(attr, dpre, precision=lax.Precision.HIGHEST, preferred_element_type=jnp.float32)
    dproj = jax.ops.segment_sum(dpre.astype(jnp.bfloat16).astype(jnp.float32), source, num_segments=GRID).astype(jnp.bfloat16)
    dw_in = jnp.dot(grid.T, dproj, preferred_element_type=jnp.float32)
    d_grid = jnp.dot(dproj, w_in.T, preferred_element_type=jnp.float32).astype(jnp.bfloat16)
    return (d_grid, d_mesh, dw_attr, dw_in, dw_out, dw_qkv, dw_o)

def reference(grid_latent, mesh_latent, edge_source, edge_dest, edge_count, edge_attr, w_attr, w_in, w_out, w_qkv, w_o, cotangent):

    def step(carry, item):
        grid, mesh, source, dest, count, attr, cot = item
        d_grid, d_mesh, dw_attr, dw_in, dw_out, dw_qkv, dw_o = one_sample(grid, mesh, source, dest, count, attr, cot, w_attr, w_in, w_out, w_qkv, w_o)
        carry = (carry[0] + dw_attr, carry[1] + dw_in, carry[2] + dw_out, carry[3] + dw_qkv, carry[4] + dw_o)
        return (carry, (d_grid, d_mesh))
    start = (jnp.zeros((ATTR, C), jnp.float32), jnp.zeros((C, C), jnp.float32), jnp.zeros((C, C), jnp.float32), jnp.zeros((3, C, C), jnp.float32), jnp.zeros((C, C), jnp.float32))
    totals, outs = lax.scan(step, start, (grid_latent, mesh_latent, edge_source, edge_dest, edge_count, edge_attr, cotangent))
    return (outs[0], outs[1], totals[0], totals[1], totals[2], totals[3], totals[4])
```

```python
import functools

import jax
import jax.numpy as jnp
from jax import lax
from jax.experimental import pallas as pl
from jax.experimental.pallas import tpu as pltpu
from jax.sharding import PartitionSpec as P

HDIM = 64


EPS = 1e-06


def shifted(block, axis, distance):
    devices = range(lax.axis_size(axis))
    route = [(i - distance, i) for i in devices if i - distance in devices]
    return lax.ppermute(block, axis, route)


def with_halo(block, sides, width):
    for axis, dim in sides:
        count = lax.axis_size(axis)
        forward = [(i, i + 1) for i in range(count - 1)]
        backward = [(target, source) for source, target in forward]
        low = lax.ppermute(
            lax.slice_in_dim(block, block.shape[dim] - width, None, axis=dim), axis, forward
        )
        high = lax.ppermute(lax.slice_in_dim(block, 0, width, axis=dim), axis, backward)
        block = jnp.concatenate([low, block, high], axis=dim)
    return block


def shards(
    grid_latent,
    mesh_latent,
    edge_source,
    edge_dest,
    edge_count,
    edge_attr,
    w_attr,
    w_in,
    w_out,
    w_qkv,
    w_o,
    cotangent,
):
    band = lax.axis_index("mp")
    grid_rows = grid_latent.shape[1]
    nodes = mesh_latent.shape[1]
    edges = edge_source.shape[1]
    grid = grid_latent[0]
    live = (jnp.arange(edges, dtype=jnp.int32) < edge_count[0, 0]).astype(jnp.float32)[:, None]
    source_local = edge_source[0] - band * grid_rows
    dest_local = edge_dest[0] - (band - 1) * nodes
    projected = jnp.dot(grid, w_in, preferred_element_type=jnp.float32)
    attr_terms = lax.dot_general(
        edge_attr[0],
        w_attr,
        (((0,), (0,)), ((), ())),
        precision=lax.Precision.HIGHEST,
        preferred_element_type=jnp.float32,
    )
    preact = projected[source_local] + attr_terms
    hidden = (jax.nn.silu(preact) * live).astype(jnp.bfloat16)
    message = jnp.dot(hidden, w_out, preferred_element_type=jnp.float32).astype(jnp.bfloat16)
    dest_table = (dest_local[:, None] == jnp.arange(3 * nodes, dtype=jnp.int32)[None, :]).astype(
        jnp.bfloat16
    )
    partial_rows = lax.dot_general(
        dest_table, message, (((0,), (0,)), ((), ())), preferred_element_type=jnp.float32
    )
    from_below = shifted(partial_rows[2 * nodes :], "mp", 1)
    from_above = shifted(partial_rows[:nodes], "mp", -1)
    node = (
        mesh_latent[0].astype(jnp.float32)
        + partial_rows[nodes : 2 * nodes]
        + from_below
        + from_above
    )
    inv = lax.rsqrt(jnp.mean(node * node, axis=-1, keepdims=True) + EPS)
    normed = (node * inv).astype(jnp.bfloat16)
    all_normed, all_cot = (
        lax.all_gather(normed, "mp", axis=0, tiled=True),
        lax.all_gather(cotangent[0], "mp", axis=0, tiled=True),
    )
    total = all_normed.shape[0]
    width = w_qkv.shape[2]
    local_heads = width // HDIM
    qkv = jnp.einsum("nc,icd->ind", all_normed, w_qkv, preferred_element_type=jnp.float32).astype(
        jnp.bfloat16
    )
    qkv = qkv.reshape(3, total, local_heads, HDIM)
    query, keys, values = (qkv[0], qkv[1], qkv[2])
    d_att = lax.dot_general(
        all_cot, w_o, (((1,), (1,)), ((), ())), preferred_element_type=jnp.float32
    ).astype(jnp.bfloat16)
    d_att = d_att.reshape(total, local_heads, HDIM)
    block = min(512, total)
    scale = HDIM ** (-0.5)

    def attend_block(carry, index):
        key_acc, value_acc = carry
        start = index * block
        query_blk = lax.dynamic_slice_in_dim(query, start, block, 0)
        grad_blk = lax.dynamic_slice_in_dim(d_att, start, block, 0)
        scores = (
            jnp.einsum("qhd,khd->hqk", query_blk, keys, preferred_element_type=jnp.float32) * scale
        )
        probs = jax.nn.softmax(scores, axis=-1)
        probs_b = probs.astype(jnp.bfloat16)
        attended = jnp.einsum(
            "hqk,khd->qhd", probs_b, values, preferred_element_type=jnp.float32
        ).astype(jnp.bfloat16)
        dprob = jnp.einsum("qhd,khd->hqk", grad_blk, values, preferred_element_type=jnp.float32)
        delta = jnp.sum(probs * dprob, axis=-1, keepdims=True)
        dscore = (probs * (dprob - delta) * scale).astype(jnp.bfloat16)
        dquery = jnp.einsum(
            "hqk,khd->qhd", dscore, keys, preferred_element_type=jnp.float32
        ).astype(jnp.bfloat16)
        key_acc = key_acc + jnp.einsum(
            "hqk,qhd->khd", dscore, query_blk, preferred_element_type=jnp.float32
        )
        value_acc = value_acc + jnp.einsum(
            "hqk,qhd->khd", probs_b, grad_blk, preferred_element_type=jnp.float32
        )
        return ((key_acc, value_acc), (attended, dquery))

    empty = jnp.zeros((total, local_heads, HDIM), jnp.float32)
    sums, blocks = lax.scan(
        attend_block, (empty, empty), jnp.arange(total // block, dtype=jnp.int32)
    )
    attended = blocks[0].reshape(total, width)
    dquery = blocks[1].reshape(total, width)
    dkeys = sums[0].astype(jnp.bfloat16).reshape(total, width)
    dvalues = sums[1].astype(jnp.bfloat16).reshape(total, width)
    dqkv = jnp.stack([dquery, dkeys, dvalues])
    dw_o = lax.dot_general(
        attended, all_cot, (((0,), (0,)), ((), ())), preferred_element_type=jnp.float32
    )
    dw_qkv = jnp.einsum("nc,ind->icd", all_normed, dqkv, preferred_element_type=jnp.float32)
    sum_qkv, sum_o = (
        lax.psum_scatter(dw_qkv.astype(jnp.bfloat16), "dp", scatter_dimension=1, tiled=True).astype(
            jnp.float32
        ),
        lax.psum_scatter(dw_o.astype(jnp.bfloat16), "dp", scatter_dimension=1, tiled=True).astype(
            jnp.float32
        ),
    )
    dx = lax.psum_scatter(
        jnp.einsum("ind,icd->nc", dqkv, w_qkv, preferred_element_type=jnp.float32).astype(
            jnp.bfloat16
        ),
        "mp",
        scatter_dimension=0,
        tiled=True,
    ).astype(jnp.float32)
    dnode = (
        cotangent[0].astype(jnp.float32)
        + inv * dx
        - node * inv * inv * inv * jnp.mean(dx * node, axis=-1, keepdims=True)
    )
    d_mesh = dnode.astype(jnp.bfloat16)
    beside_all = with_halo(d_mesh, (("mp", 0),), nodes)
    dmessage = (beside_all[dest_local].astype(jnp.float32) * live).astype(jnp.bfloat16)
    dw_out = lax.dot_general(
        hidden, dmessage, (((0,), (0,)), ((), ())), preferred_element_type=jnp.float32
    )
    dhidden = lax.dot_general(
        dmessage, w_out, (((1,), (1,)), ((), ())), preferred_element_type=jnp.float32
    )
    sigma = jax.nn.sigmoid(preact)
    dpre = dhidden * sigma * (1.0 + preact * (1.0 - sigma)) * live
    dw_attr = jnp.dot(
        edge_attr[0], dpre, precision=lax.Precision.HIGHEST, preferred_element_type=jnp.float32
    )
    source_table = (
        source_local[:, None] == jnp.arange(grid_rows, dtype=jnp.int32)[None, :]
    ).astype(jnp.bfloat16)
    dproj = lax.dot_general(
        source_table,
        dpre.astype(jnp.bfloat16),
        (((0,), (0,)), ((), ())),
        preferred_element_type=jnp.float32,
    ).astype(jnp.bfloat16)
    dw_in = lax.dot_general(
        grid, dproj, (((0,), (0,)), ((), ())), preferred_element_type=jnp.float32
    )
    d_grid = lax.dot_general(
        dproj, w_in, (((1,), (1,)), ((), ())), preferred_element_type=jnp.float32
    ).astype(jnp.bfloat16)
    sum_attr = lax.psum(dw_attr, ("dp", "mp"))
    first_in, first_out = (
        lax.psum_scatter(dw_in.astype(jnp.bfloat16), "dp", scatter_dimension=0, tiled=True).astype(
            jnp.float32
        ),
        lax.psum_scatter(dw_out.astype(jnp.bfloat16), "dp", scatter_dimension=0, tiled=True).astype(
            jnp.float32
        ),
    )
    sum_in, sum_out = (
        lax.psum_scatter(
            first_in.astype(jnp.bfloat16), "mp", scatter_dimension=1, tiled=True
        ).astype(jnp.float32),
        lax.psum_scatter(
            first_out.astype(jnp.bfloat16), "mp", scatter_dimension=1, tiled=True
        ).astype(jnp.float32),
    )
    return (d_grid[None], d_mesh[None], sum_attr, sum_in, sum_out, sum_qkv, sum_o)


F32 = jnp.float32
BF16 = jnp.bfloat16
LANES = 128
TILE = 256


def nn(a, b):
    return jnp.dot(a, b, preferred_element_type=F32)


def nt(a, b):
    return lax.dot_general(a, b, (((1,), (1,)), ((), ())), preferred_element_type=F32)


def tn(a, b):
    return lax.dot_general(a, b, (((0,), (0,)), ((), ())), preferred_element_type=F32)


def span(index, size):
    return pl.ds(pl.multiple_of(index * size, size), size)


def loop(count, body):
    def step(i, carry):
        body(i)
        return carry

    lax.fori_loop(0, count, step, 0)


def layer_kernel(
    n_mp,
    grid_ref,
    mesh_ref,
    icol_ref,
    irow_ref,
    aux_ref,
    w_attr_ref,
    w_in_ref,
    w_out_ref,
    w_qkv_ref,
    w_o_ref,
    cot_ref,
    d_grid_ref,
    d_mesh_ref,
    d_attr_ref,
    d_in_ref,
    d_out_ref,
    d_qkv_ref,
    d_o_ref,
    split_ref,
    pre_ref,
    hid_ref,
    msg_ref,
    hsend,
    hrecv,
    node_ref,
    x_all,
    cot_all,
    qkvg,
    dqkv,
    att_ref,
    dxs,
    dxr,
    beside,
    dproj_ref,
    parts,
    r1,
    r2,
    r3,
    mpb,
    mpr,
    at_own,
    at_recv,
    at_all,
    cot_sem,
    x_sem,
    halo_sem,
    dx_sem,
    beside_sem,
    rs_sem,
    mp_sem,
    at_sem,
):
    d = lax.axis_index("dp")
    me = lax.axis_index("mp")
    core = d % 2
    px = (d // 2) % 2
    py = d // 4
    by_core = (d + 1 - 2 * core, me)
    by_x = (d + 2 - 4 * px, me)
    by_y = (d + 4 - 8 * py, me)
    second = (by_x[0] * (1 - core) + by_y[0] * core, me)
    third = (by_y[0] * (1 - core) + by_x[0] * core, me)

    def along(offset):
        return (d, (me + offset + n_mp) % n_mp)

    grid_rows, c = grid_ref.shape
    nodes = mesh_ref.shape[0]
    edges = aux_ref.shape[0]
    attrs = w_attr_ref.shape[0]
    width = w_o_ref.shape[0]
    total = nodes * n_mp
    rows = parts.shape[3]
    cols = mpb.shape[3]
    scale = HDIM ** (-0.5)
    chunks = edges // TILE

    def copy(src, dst, sems, to):
        return pltpu.make_async_remote_copy(
            src_ref=src,
            dst_ref=dst,
            send_sem=sems.at[0],
            recv_sem=sems.at[1],
            device_id=to,
            device_id_type=pl.DeviceIdType.MESH,
        )

    barrier = pltpu.get_barrier_semaphore()
    greeted = [by_core, by_x, by_y] + [along(o) for o in range(1, n_mp)]
    for other in greeted:
        pl.semaphore_signal(
            barrier, inc=1, device_id=other, device_id_type=pl.DeviceIdType.MESH
        )
    pl.semaphore_wait(barrier, len(greeted))

    def block(o):
        return pl.ds(o * nodes, nodes)

    cot_copies = [
        copy(cot_ref, cot_all.at[block(o)], cot_sem.at[o - 1], along(o)) for o in range(1, n_mp)
    ]
    for one in cot_copies:
        one.start()
    cot_all[block(0), :] = cot_ref[...]

    def project(j):
        at = span(j, 2 * TILE)
        value = nn(grid_ref[...], w_in_ref[:, at])
        high = value.astype(BF16)
        split_ref[pl.ds(0, grid_rows), at] = high
        split_ref[pl.ds(grid_rows, grid_rows), at] = (value - high.astype(F32)).astype(BF16)

    loop(c // (2 * TILE), project)

    def edge_forward(i):
        at = span(i, TILE)
        source = icol_ref[at, 0:1]
        place = lax.broadcasted_iota(jnp.int32, (TILE, grid_rows), 1)
        table = (source == place).astype(F32).astype(BF16)
        table = jnp.concatenate([table, table], axis=1)
        aux = aux_ref[at, :]
        pre = nn(table, split_ref[...])
        for a in range(attrs):
            pre = pre + aux[:, a : a + 1] * w_attr_ref[a : a + 1, :]
        pre_ref[at, :] = pre
        hidden = (pre / (1.0 + jnp.exp(-pre)) * aux[:, attrs : attrs + 1]).astype(BF16)
        hid_ref[at, :] = hidden
        msg_ref[at, :] = nn(hidden, w_out_ref[...]).astype(BF16)

    loop(chunks, edge_forward)

    dest = irow_ref[1:2, :]
    place = lax.broadcasted_iota(jnp.int32, (2 * nodes, edges), 0)
    place = jnp.where(place < nodes, place, place + nodes)
    sides = nn((dest == place).astype(F32).astype(BF16), msg_ref[...])
    hsend[0] = sides[:nodes].astype(BF16)
    hsend[1] = sides[nodes:].astype(BF16)
    down = copy(hsend.at[0], hrecv.at[1], halo_sem.at[0], along(-1))
    up = copy(hsend.at[1], hrecv.at[0], halo_sem.at[1], along(1))
    first, last = me == 0, me == n_mp - 1

    def exchange(lower, upper, low_slot, high_slot):
        @pl.when(jnp.logical_not(first))
        def _():
            lower.start()

        @pl.when(jnp.logical_not(last))
        def _():
            upper.start()

        @pl.when(first)
        def _():
            low_slot[...] = jnp.zeros_like(low_slot)

        @pl.when(last)
        def _():
            high_slot[...] = jnp.zeros_like(high_slot)

    def settle(lower, upper):
        @pl.when(jnp.logical_not(first))
        def _():
            lower.wait_send()
            upper.wait_recv()

        @pl.when(jnp.logical_not(last))
        def _():
            upper.wait_send()
            lower.wait_recv()

    exchange(down, up, hrecv.at[0], hrecv.at[1])
    place = lax.broadcasted_iota(jnp.int32, (nodes, edges), 0) + nodes
    node = mesh_ref[...].astype(F32) + nn(
        (dest == place).astype(F32).astype(BF16), msg_ref[...]
    )
    settle(down, up)
    node = node + hrecv[0].astype(F32) + hrecv[1].astype(F32)
    inv = lax.rsqrt(jnp.mean(node * node, axis=-1, keepdims=True) + EPS)
    node_ref[...] = node
    x_all[block(0), :] = (node * inv).astype(BF16)

    x_copies = [
        copy(x_all.at[block(0)], x_all.at[block(o)], x_sem.at[o - 1], along(o))
        for o in range(1, n_mp)
    ]
    for one in x_copies:
        one.start()

    def qkv(o):
        band = x_all[block(o), :]
        for i in range(3):
            qkvg[i, block(o), :] = nn(band, w_qkv_ref[i]).astype(BF16)

    qkv(0)
    for one in cot_copies:
        one.wait()
    qkvg[3] = nt(cot_all[...], w_o_ref[...]).astype(BF16)
    nearest = sorted(range(1, n_mp), key=lambda o: min(o, n_mp - o))
    for o in nearest:
        x_copies[o - 1].wait()
        qkv(o)

    lane = lax.broadcasted_iota(jnp.int32, (1, LANES), 1)

    def heads(p):
        at = span(p, LANES)
        q, k, v, g = (qkvg[i, :, at] for i in range(4))
        sums = [jnp.zeros((total, LANES), F32) for _ in range(4)]
        for h in range(LANES // HDIM):
            own = jnp.logical_and(lane >= h * HDIM, lane < (h + 1) * HDIM)
            own = own.astype(F32).astype(BF16)
            qh, kh, vh, gh = q * own, k * own, v * own, g * own
            scores = nt(qh, k) * scale
            probs = jnp.exp(scores - jnp.max(scores, axis=-1, keepdims=True))
            probs = probs * (1.0 / jnp.sum(probs, axis=-1, keepdims=True))
            probs_b = probs.astype(BF16)
            dprob = nt(gh, v)
            delta = jnp.sum(probs * dprob, axis=-1, keepdims=True)
            dscore = (probs * (dprob - delta) * scale).astype(BF16)
            sums[0] = sums[0] + nn(dscore, kh)
            sums[1] = sums[1] + tn(dscore, qh)
            sums[2] = sums[2] + tn(probs_b, gh)
            sums[3] = sums[3] + nn(probs_b, vh)
        for i in range(3):
            dqkv[i, :, at] = sums[i].astype(BF16)
        att_ref[:, at] = sums[3].astype(BF16)

    loop(width // LANES, heads)

    dx_copies = [
        copy(dxs.at[block(o)], dxr.at[o - 1], dx_sem.at[o - 1], along(-o)) for o in range(1, n_mp)
    ]
    half = n_mp // 2
    for start in (half, 0):
        at = pl.ds(start * nodes, half * nodes)
        value = nt(dqkv[0, at, :], w_qkv_ref[0])
        value = value + nt(dqkv[1, at, :], w_qkv_ref[1])
        value = value + nt(dqkv[2, at, :], w_qkv_ref[2])
        dxs[at, :] = value.astype(BF16)
        for o in range(max(start, 1), start + half):
            dx_copies[o - 1].start()

    def keep(j):
        return (j * 2 + px) * (1 - core) + (py * 2 + j) * core

    def give(j):
        return (j * 2 + 1 - px) * (1 - core) + ((1 - py) * 2 + j) * core

    def stage(group, number):
        sems = rs_sem.at[group]
        mine = parts.at[group]
        if number == 0:
            return [copy(mine.at[1 - core], r1.at[group], sems.at[0], by_core)]
        if number == 1:
            return [
                copy(mine.at[core, give(j)], r2.at[group, j], sems.at[1 + j], second)
                for j in range(2)
            ]
        rest = (1 - py) * (1 - core) + (1 - px) * core
        return [copy(mine.at[core, keep(rest)], r3.at[group], sems.at[3], third)]

    def begin(group, number):
        for one in stage(group, number):
            one.start()

    def add(group, slot, other):
        value = parts[group, core, slot].astype(F32) + other.astype(F32)
        parts[group, core, slot] = value.astype(BF16)

    def finish_first(group):
        for one in stage(group, 0):
            one.wait()
        for j in range(2):
            add(group, give(j), r1[group, give(j)])
        begin(group, 1)
        for j in range(2):
            add(group, keep(j), r1[group, keep(j)])

    def finish_second(group):
        for one in stage(group, 1):
            one.wait()
        rest = (1 - py) * (1 - core) + (1 - px) * core
        add(group, keep(rest), r2[group, rest])
        begin(group, 2)
        add(group, keep(1 - rest), r2[group, 1 - rest])

    def finish_third(group):
        for one in stage(group, 2):
            one.wait()
        return parts[group, core, py * 2 + px].astype(F32) + r3[group].astype(F32)

    def pairs(fill):
        loop(parts.shape[2], fill)

    def fill_qkv(j):
        at = span(j, 2 * rows)
        x_part = x_all[:, at]
        for i in range(3):
            value = tn(x_part, dqkv[i]).astype(BF16)
            for side in range(2):
                parts[0, side, j, :, pl.ds(i * width, width)] = value[side * rows : (side + 1) * rows]
        value = tn(cot_all[:, at], att_ref[...]).astype(BF16)
        for side in range(2):
            parts[0, side, j, :, pl.ds(3 * width, width)] = value[side * rows : (side + 1) * rows]

    pairs(fill_qkv)
    begin(0, 0)

    for one in dx_copies:
        one.wait()
    dx = dxs[block(0), :].astype(F32)
    for o in range(1, n_mp):
        dx = dx + dxr[o - 1].astype(F32)
    node = node_ref[...]
    inv = lax.rsqrt(jnp.mean(node * node, axis=-1, keepdims=True) + EPS)
    mean = jnp.mean(dx * node, axis=-1, keepdims=True)
    dnode = cot_ref[...].astype(F32) + inv * dx - node * inv * inv * inv * mean
    beside[pl.ds(nodes, nodes), :] = dnode.astype(BF16)
    middle = beside.at[pl.ds(nodes, nodes)]
    low, high = beside.at[pl.ds(0, nodes)], beside.at[pl.ds(2 * nodes, nodes)]
    down = copy(middle, high, beside_sem.at[0], along(-1))
    up = copy(middle, low, beside_sem.at[1], along(1))
    exchange(down, up, low, high)
    d_mesh_ref[...] = dnode.astype(BF16)
    finish_first(0)
    settle(down, up)

    def edge_gather(i):
        at = span(i, TILE)
        place = lax.broadcasted_iota(jnp.int32, (TILE, 3 * nodes), 1)
        table = (icol_ref[at, 1:2] == place).astype(F32) * aux_ref[at, attrs : attrs + 1]
        msg_ref[at, :] = nn(table.astype(BF16), beside[...]).astype(BF16)

    loop(chunks, edge_gather)

    def fill_out(j):
        value = tn(hid_ref[:, span(j, 2 * rows)], msg_ref[...]).astype(BF16)
        for side in range(2):
            parts[1, side, j] = value[side * rows : (side + 1) * rows]

    pairs(fill_out)
    begin(1, 0)
    finish_second(0)

    at_own[...] = jnp.zeros_like(at_own)

    def edge_backward(i):
        at = span(i, TILE)
        aux = aux_ref[at, :]
        pre = pre_ref[at, :]
        sigma = 1.0 / (1.0 + jnp.exp(-pre))
        dpre = nt(msg_ref[at, :], w_out_ref[...])
        dpre = dpre * sigma * (1.0 + pre * (1.0 - sigma)) * aux[:, attrs : attrs + 1]
        for a in range(attrs):
            at_own[a : a + 1, :] += jnp.sum(aux[:, a : a + 1] * dpre, axis=0, keepdims=True)
        msg_ref[at, :] = dpre.astype(BF16)

    loop(chunks, edge_backward)
    finish_first(1)

    attr_steps = [
        copy(at_own, at_recv.at[i], at_sem.at[i], to) for i, to in enumerate((by_core, by_x, by_y))
    ]
    attr_steps[0].start()
    place = lax.broadcasted_iota(jnp.int32, (grid_rows, edges), 0)
    table = (irow_ref[0:1, :] == place).astype(F32).astype(BF16)
    dproj_ref[...] = nn(table, msg_ref[...]).astype(BF16)

    def fill_in(j):
        value = tn(grid_ref[:, span(j, 2 * rows)], dproj_ref[...]).astype(BF16)
        for side in range(2):
            parts[2, side, j] = value[side * rows : (side + 1) * rows]

    pairs(fill_in)
    begin(2, 0)
    finish_second(1)
    attr_steps[0].wait()
    at_own[...] = at_own[...] + at_recv[0]
    attr_steps[1].start()

    def grid_back(j):
        at = span(j, 2 * TILE)
        d_grid_ref[:, at] = nt(dproj_ref[...], w_in_ref[at, :]).astype(BF16)

    finish_first(2)
    loop(c // (2 * TILE), grid_back)

    value = finish_third(0)
    for i in range(3):
        d_qkv_ref[i] = value[:, i * width : (i + 1) * width]
    d_o_ref[...] = value[:, 3 * width :].T
    attr_steps[1].wait()
    at_own[...] = at_own[...] + at_recv[1]
    attr_steps[2].start()

    def spread(group):
        value = finish_third(group)
        for t in range(n_mp):
            mpb[group - 1, t] = value[:, t * cols : (t + 1) * cols].astype(BF16)
        copies = [
            copy(
                mpb.at[group - 1, (me + o) % n_mp],
                mpr.at[group - 1, o - 1],
                mp_sem.at[group - 1, o - 1],
                along(o),
            )
            for o in range(1, n_mp)
        ]
        for one in copies:
            one.start()
        return copies

    def collect(group, copies, out_ref):
        for one in copies:
            one.wait()
        value = mpb[group - 1, me].astype(F32)
        for o in range(1, n_mp):
            value = value + mpr[group - 1, o - 1].astype(F32)
        out_ref[...] = value

    out_copies = spread(1)
    finish_second(2)
    attr_steps[2].wait()
    at_all[0] = at_own[...] + at_recv[2]
    attr_copies = [
        copy(at_all.at[0], at_all.at[o], at_sem.at[2 + o], along(o)) for o in range(1, n_mp)
    ]
    for one in attr_copies:
        one.start()
    in_copies = spread(2)
    for one in attr_copies:
        one.wait()
    value = at_all[me]
    for s in range(1, n_mp):
        value = value + at_all[(me + n_mp - s) % n_mp]
    d_attr_ref[...] = value
    collect(1, out_copies, d_out_ref)
    collect(2, in_copies, d_in_ref)


def fused(
    grid_latent,
    mesh_latent,
    edge_source,
    edge_dest,
    edge_count,
    edge_attr,
    w_attr,
    w_in,
    w_out,
    w_qkv,
    w_o,
    cotangent,
):
    n_dp, n_mp = lax.axis_size("dp"), lax.axis_size("mp")
    band = lax.axis_index("mp")
    grid_rows, c = grid_latent.shape[1:]
    nodes = mesh_latent.shape[1]
    edges = edge_source.shape[1]
    attrs = w_attr.shape[0]
    width = w_qkv.shape[2]
    total = nodes * n_mp
    rows, cols = c // n_dp, c // n_mp
    live = (jnp.arange(edges, dtype=jnp.int32) < edge_count[0, 0]).astype(F32)
    irow = jnp.concatenate([edge_source - band * grid_rows, edge_dest - (band - 1) * nodes], axis=0)
    aux = jnp.concatenate([edge_attr[0], live[None]], axis=0).T
    vmem = pl.BlockSpec(memory_space=pltpu.VMEM)
    shape = jax.ShapeDtypeStruct
    dma = pltpu.SemaphoreType.DMA
    outs = pl.pallas_call(
        functools.partial(layer_kernel, n_mp),
        out_shape=(
            shape((grid_rows, c), BF16),
            shape((nodes, c), BF16),
            shape((attrs, c), F32),
            shape((rows, cols), F32),
            shape((rows, cols), F32),
            shape((3, rows, width), F32),
            shape((width, rows), F32),
        ),
        in_specs=[vmem] * 11,
        out_specs=[vmem] * 7,
        scratch_shapes=[
            pltpu.VMEM((2 * grid_rows, c), BF16),
            pltpu.VMEM((edges, c), F32),
            pltpu.VMEM((edges, c), BF16),
            pltpu.VMEM((edges, c), BF16),
            pltpu.VMEM((2, nodes, c), BF16),
            pltpu.VMEM((2, nodes, c), BF16),
            pltpu.VMEM((nodes, c), F32),
            pltpu.VMEM((total, c), BF16),
            pltpu.VMEM((total, c), BF16),
            pltpu.VMEM((4, total, width), BF16),
            pltpu.VMEM((3, total, width), BF16),
            pltpu.VMEM((total, width), BF16),
            pltpu.VMEM((total, c), BF16),
            pltpu.VMEM((n_mp - 1, nodes, c), BF16),
            pltpu.VMEM((3 * nodes, c), BF16),
            pltpu.VMEM((grid_rows, c), BF16),
            pltpu.VMEM((3, 2, n_dp // 2, rows, c), BF16),
            pltpu.VMEM((3, n_dp // 2, rows, c), BF16),
            pltpu.VMEM((3, 2, rows, c), BF16),
            pltpu.VMEM((3, rows, c), BF16),
            pltpu.VMEM((2, n_mp, rows, cols), BF16),
            pltpu.VMEM((2, n_mp - 1, rows, cols), BF16),
            pltpu.VMEM((attrs, c), F32),
            pltpu.VMEM((3, attrs, c), F32),
            pltpu.VMEM((n_mp, attrs, c), F32),
            dma((n_mp - 1, 2)),
            dma((n_mp - 1, 2)),
            dma((2, 2)),
            dma((n_mp - 1, 2)),
            dma((2, 2)),
            dma((3, 4, 2)),
            dma((2, n_mp - 1, 2)),
            dma((2 + n_mp, 2)),
        ],
        compiler_params=pltpu.CompilerParams(
            collective_id=0, has_side_effects=True, vmem_limit_bytes=58 * 2**20
        ),
    )(
        grid_latent[0],
        mesh_latent[0],
        irow.T,
        irow,
        aux,
        w_attr,
        w_in,
        w_out,
        w_qkv,
        w_o,
        cotangent[0],
    )
    return (outs[0][None], outs[1][None]) + tuple(outs[2:])


def step(*arrays):
    grid_latent, mesh_latent, edge_source, w_qkv = (arrays[i] for i in (0, 1, 2, 9))
    c, width = w_qkv.shape[1:]
    n_dp, n_mp = lax.axis_size("dp"), lax.axis_size("mp")
    fits = (
        n_dp == 8
        and n_mp % 2 == 0
        and n_mp * mesh_latent.shape[1] <= 512
        and 4 * width == c
        and width % LANES == 0
        and c % (2 * TILE) == 0
        and (c // n_dp) % LANES == 0
        and edge_source.shape[1] % TILE == 0
        and grid_latent.shape[1] % LANES == 0
    )
    return fused(*arrays) if fits else shards(*arrays)


def solution(mesh):
    return jax.shard_map(
        step,
        mesh=mesh,
        in_specs=(
            P("dp", "mp", None),
            P("dp", "mp", None),
            P("dp", "mp"),
            P("dp", "mp"),
            P("dp", "mp"),
            P("dp", None, "mp"),
            P(),
            P(),
            P(),
            P(None, None, "mp"),
            P("mp", None),
            P("dp", "mp", None),
        ),
        out_specs=(
            P("dp", "mp", None),
            P("dp", "mp", None),
            P(),
            P("dp", "mp"),
            P("dp", "mp"),
            P(None, "dp", "mp"),
            P("mp", "dp"),
        ),
        check_vma=False,
    )
```

```python
import functools

import jax
import jax.numpy as jnp
from jax import lax
from jax.experimental import pallas as pl
from jax.experimental.pallas import tpu as pltpu
from jax.sharding import PartitionSpec as P

HDIM = 64


EPS = 1e-06


def shifted(block, axis, distance):
    devices = range(lax.axis_size(axis))
    route = [(i - distance, i) for i in devices if i - distance in devices]
    return lax.ppermute(block, axis, route)


def with_halo(block, sides, width):
    for axis, dim in sides:
        count = lax.axis_size(axis)
        forward = [(i, i + 1) for i in range(count - 1)]
        backward = [(target, source) for source, target in forward]
        low = lax.ppermute(
            lax.slice_in_dim(block, block.shape[dim] - width, None, axis=dim), axis, forward
        )
        high = lax.ppermute(lax.slice_in_dim(block, 0, width, axis=dim), axis, backward)
        block = jnp.concatenate([low, block, high], axis=dim)
    return block


def shards(
    grid_latent,
    mesh_latent,
    edge_source,
    edge_dest,
    edge_count,
    edge_attr,
    w_attr,
    w_in,
    w_out,
    w_qkv,
    w_o,
    cotangent,
):
    band = lax.axis_index("mp")
    grid_rows = grid_latent.shape[1]
    nodes = mesh_latent.shape[1]
    edges = edge_source.shape[1]
    grid = grid_latent[0]
    live = (jnp.arange(edges, dtype=jnp.int32) < edge_count[0, 0]).astype(jnp.float32)[:, None]
    source_local = edge_source[0] - band * grid_rows
    dest_local = edge_dest[0] - (band - 1) * nodes
    projected = jnp.dot(grid, w_in, preferred_element_type=jnp.float32)
    attr_terms = lax.dot_general(
        edge_attr[0],
        w_attr,
        (((0,), (0,)), ((), ())),
        precision=lax.Precision.HIGHEST,
        preferred_element_type=jnp.float32,
    )
    preact = projected[source_local] + attr_terms
    hidden = (jax.nn.silu(preact) * live).astype(jnp.bfloat16)
    message = jnp.dot(hidden, w_out, preferred_element_type=jnp.float32).astype(jnp.bfloat16)
    dest_table = (dest_local[:, None] == jnp.arange(3 * nodes, dtype=jnp.int32)[None, :]).astype(
        jnp.bfloat16
    )
    partial_rows = lax.dot_general(
        dest_table, message, (((0,), (0,)), ((), ())), preferred_element_type=jnp.float32
    )
    from_below = shifted(partial_rows[2 * nodes :], "mp", 1)
    from_above = shifted(partial_rows[:nodes], "mp", -1)
    node = (
        mesh_latent[0].astype(jnp.float32)
        + partial_rows[nodes : 2 * nodes]
        + from_below
        + from_above
    )
    inv = lax.rsqrt(jnp.mean(node * node, axis=-1, keepdims=True) + EPS)
    normed = (node * inv).astype(jnp.bfloat16)
    all_normed, all_cot = (
        lax.all_gather(normed, "mp", axis=0, tiled=True),
        lax.all_gather(cotangent[0], "mp", axis=0, tiled=True),
    )
    total = all_normed.shape[0]
    width = w_qkv.shape[2]
    local_heads = width // HDIM
    qkv = jnp.einsum("nc,icd->ind", all_normed, w_qkv, preferred_element_type=jnp.float32).astype(
        jnp.bfloat16
    )
    qkv = qkv.reshape(3, total, local_heads, HDIM)
    query, keys, values = (qkv[0], qkv[1], qkv[2])
    d_att = lax.dot_general(
        all_cot, w_o, (((1,), (1,)), ((), ())), preferred_element_type=jnp.float32
    ).astype(jnp.bfloat16)
    d_att = d_att.reshape(total, local_heads, HDIM)
    block = min(512, total)
    scale = HDIM ** (-0.5)

    def attend_block(carry, index):
        key_acc, value_acc = carry
        start = index * block
        query_blk = lax.dynamic_slice_in_dim(query, start, block, 0)
        grad_blk = lax.dynamic_slice_in_dim(d_att, start, block, 0)
        scores = (
            jnp.einsum("qhd,khd->hqk", query_blk, keys, preferred_element_type=jnp.float32) * scale
        )
        probs = jax.nn.softmax(scores, axis=-1)
        probs_b = probs.astype(jnp.bfloat16)
        attended = jnp.einsum(
            "hqk,khd->qhd", probs_b, values, preferred_element_type=jnp.float32
        ).astype(jnp.bfloat16)
        dprob = jnp.einsum("qhd,khd->hqk", grad_blk, values, preferred_element_type=jnp.float32)
        delta = jnp.sum(probs * dprob, axis=-1, keepdims=True)
        dscore = (probs * (dprob - delta) * scale).astype(jnp.bfloat16)
        dquery = jnp.einsum(
            "hqk,khd->qhd", dscore, keys, preferred_element_type=jnp.float32
        ).astype(jnp.bfloat16)
        key_acc = key_acc + jnp.einsum(
            "hqk,qhd->khd", dscore, query_blk, preferred_element_type=jnp.float32
        )
        value_acc = value_acc + jnp.einsum(
            "hqk,qhd->khd", probs_b, grad_blk, preferred_element_type=jnp.float32
        )
        return ((key_acc, value_acc), (attended, dquery))

    empty = jnp.zeros((total, local_heads, HDIM), jnp.float32)
    sums, blocks = lax.scan(
        attend_block, (empty, empty), jnp.arange(total // block, dtype=jnp.int32)
    )
    attended = blocks[0].reshape(total, width)
    dquery = blocks[1].reshape(total, width)
    dkeys = sums[0].astype(jnp.bfloat16).reshape(total, width)
    dvalues = sums[1].astype(jnp.bfloat16).reshape(total, width)
    dqkv = jnp.stack([dquery, dkeys, dvalues])
    dw_o = lax.dot_general(
        attended, all_cot, (((0,), (0,)), ((), ())), preferred_element_type=jnp.float32
    )
    dw_qkv = jnp.einsum("nc,ind->icd", all_normed, dqkv, preferred_element_type=jnp.float32)
    sum_qkv, sum_o = (
        lax.psum_scatter(dw_qkv.astype(jnp.bfloat16), "dp", scatter_dimension=1, tiled=True).astype(
            jnp.float32
        ),
        lax.psum_scatter(dw_o.astype(jnp.bfloat16), "dp", scatter_dimension=1, tiled=True).astype(
            jnp.float32
        ),
    )
    dx = lax.psum_scatter(
        jnp.einsum("ind,icd->nc", dqkv, w_qkv, preferred_element_type=jnp.float32).astype(
            jnp.bfloat16
        ),
        "mp",
        scatter_dimension=0,
        tiled=True,
    ).astype(jnp.float32)
    dnode = (
        cotangent[0].astype(jnp.float32)
        + inv * dx
        - node * inv * inv * inv * jnp.mean(dx * node, axis=-1, keepdims=True)
    )
    d_mesh = dnode.astype(jnp.bfloat16)
    beside_all = with_halo(d_mesh, (("mp", 0),), nodes)
    dmessage = (beside_all[dest_local].astype(jnp.float32) * live).astype(jnp.bfloat16)
    dw_out = lax.dot_general(
        hidden, dmessage, (((0,), (0,)), ((), ())), preferred_element_type=jnp.float32
    )
    dhidden = lax.dot_general(
        dmessage, w_out, (((1,), (1,)), ((), ())), preferred_element_type=jnp.float32
    )
    sigma = jax.nn.sigmoid(preact)
    dpre = dhidden * sigma * (1.0 + preact * (1.0 - sigma)) * live
    dw_attr = jnp.dot(
        edge_attr[0], dpre, precision=lax.Precision.HIGHEST, preferred_element_type=jnp.float32
    )
    source_table = (
        source_local[:, None] == jnp.arange(grid_rows, dtype=jnp.int32)[None, :]
    ).astype(jnp.bfloat16)
    dproj = lax.dot_general(
        source_table,
        dpre.astype(jnp.bfloat16),
        (((0,), (0,)), ((), ())),
        preferred_element_type=jnp.float32,
    ).astype(jnp.bfloat16)
    dw_in = lax.dot_general(
        grid, dproj, (((0,), (0,)), ((), ())), preferred_element_type=jnp.float32
    )
    d_grid = lax.dot_general(
        dproj, w_in, (((1,), (1,)), ((), ())), preferred_element_type=jnp.float32
    ).astype(jnp.bfloat16)
    sum_attr = lax.psum(dw_attr, ("dp", "mp"))
    first_in, first_out = (
        lax.psum_scatter(dw_in.astype(jnp.bfloat16), "dp", scatter_dimension=0, tiled=True).astype(
            jnp.float32
        ),
        lax.psum_scatter(dw_out.astype(jnp.bfloat16), "dp", scatter_dimension=0, tiled=True).astype(
            jnp.float32
        ),
    )
    sum_in, sum_out = (
        lax.psum_scatter(
            first_in.astype(jnp.bfloat16), "mp", scatter_dimension=1, tiled=True
        ).astype(jnp.float32),
        lax.psum_scatter(
            first_out.astype(jnp.bfloat16), "mp", scatter_dimension=1, tiled=True
        ).astype(jnp.float32),
    )
    return (d_grid[None], d_mesh[None], sum_attr, sum_in, sum_out, sum_qkv, sum_o)


F32 = jnp.float32
BF16 = jnp.bfloat16
LANES = 128
TILE = 256


def nn(a, b):
    return jnp.dot(a, b, preferred_element_type=F32)


def nt(a, b):
    return lax.dot_general(a, b, (((1,), (1,)), ((), ())), preferred_element_type=F32)


def tn(a, b):
    return lax.dot_general(a, b, (((0,), (0,)), ((), ())), preferred_element_type=F32)


def span(index, size):
    return pl.ds(pl.multiple_of(index * size, size), size)


def loop(count, body):
    def step(i, carry):
        body(i)
        return carry

    lax.fori_loop(0, count, step, 0)


def layer_kernel(
    n_mp,
    grid_ref,
    mesh_ref,
    source_ref,
    dest_ref,
    count_ref,
    attr_ref,
    w_attr_ref,
    w_in_ref,
    w_out_ref,
    w_qkv_ref,
    w_o_ref,
    cot_ref,
    d_grid_ref,
    d_mesh_ref,
    d_attr_ref,
    d_in_ref,
    d_out_ref,
    d_qkv_ref,
    d_o_ref,
    split_ref,
    slope_ref,
    hid_ref,
    hid_t,
    grid_t,
    msg_ref,
    row_ref,
    col_ref,
    hsend,
    hrecv,
    node_ref,
    x_all,
    cot_all,
    qkvg,
    dqkv,
    att_ref,
    dxs,
    dxr,
    beside,
    dproj_ref,
    parts,
    r1,
    r2,
    r3,
    mpb,
    mpr,
    at_own,
    at_recv,
    at_all,
    cot_sem,
    x_sem,
    halo_sem,
    dx_sem,
    beside_sem,
    rs_sem,
    mp_sem,
    at_sem,
):
    d = lax.axis_index("dp")
    me = lax.axis_index("mp")
    core = d % 2
    px = (d // 2) % 2
    py = d // 4
    by_core = (d + 1 - 2 * core, me)
    by_x = (d + 2 - 4 * px, me)
    by_y = (d + 4 - 8 * py, me)
    second = (by_x[0] * (1 - core) + by_y[0] * core, me)
    third = (by_y[0] * (1 - core) + by_x[0] * core, me)

    def along(offset):
        return (d, (me + offset + n_mp) % n_mp)

    grid_rows, c = grid_ref.shape
    nodes = mesh_ref.shape[0]
    edges = source_ref.shape[1]
    attrs = w_attr_ref.shape[0]
    width = w_o_ref.shape[0]
    total = nodes * n_mp
    rows = parts.shape[3]
    cols = mpb.shape[3]
    scale = HDIM ** (-0.5)
    chunks = edges // TILE

    def copy(src, dst, sems, to):
        return pltpu.make_async_remote_copy(
            src_ref=src,
            dst_ref=dst,
            send_sem=sems.at[0],
            recv_sem=sems.at[1],
            device_id=to,
            device_id_type=pl.DeviceIdType.MESH,
        )

    barrier = pltpu.get_barrier_semaphore()
    greeted = [by_core, by_x, by_y] + [along(o) for o in range(1, n_mp)]
    for other in greeted:
        pl.semaphore_signal(
            barrier, inc=1, device_id=other, device_id_type=pl.DeviceIdType.MESH
        )
    pl.semaphore_wait(barrier, len(greeted))

    def block(o):
        return pl.ds(o * nodes, nodes)

    first, last = me == 0, me == n_mp - 1

    def relay(blocks, sems):
        def right(t):
            return copy(blocks.at[block(t)], blocks.at[block(t + 1)], sems.at[0, t], along(1))

        def left(t):
            return copy(
                blocks.at[block((n_mp - t) % n_mp)],
                blocks.at[block(n_mp - t - 1)],
                sems.at[1, t],
                along(-1),
            )

        def send(t):
            @pl.when(jnp.logical_and(me >= t, jnp.logical_not(last)))
            def _():
                right(t).start()

            @pl.when(jnp.logical_and(me + t <= n_mp - 1, jnp.logical_not(first)))
            def _():
                left(t).start()

        def hop(t, use=None):
            @pl.when(me >= t)
            def _():
                right(t - 1).wait_recv()

            @pl.when(me + t <= n_mp - 1)
            def _():
                left(t - 1).wait_recv()

            if t < n_mp - 1:
                send(t)
            if use is not None:

                @pl.when(me >= t)
                def _():
                    use(t)

                @pl.when(me + t <= n_mp - 1)
                def _():
                    use(n_mp - t)

        def drain():
            for t in range(n_mp - 1):

                @pl.when(jnp.logical_and(me >= t, jnp.logical_not(last)))
                def _(t=t):
                    right(t).wait_send()

                @pl.when(jnp.logical_and(me + t <= n_mp - 1, jnp.logical_not(first)))
                def _(t=t):
                    left(t).wait_send()

        return send, hop, drain

    cot_all[block(0), :] = cot_ref[...]
    cot_send, cot_hop, cot_drain = relay(cot_all, cot_sem)
    cot_send(0)

    row_ref[...] = jnp.zeros_like(row_ref)
    row_ref[0:1, :] = (source_ref[...] - me * grid_rows).astype(F32)
    row_ref[1:2, :] = (dest_ref[...] - (me - 1) * nodes).astype(F32)
    position = lax.broadcasted_iota(jnp.int32, (1, edges), 1)
    row_ref[2:3, :] = (position < count_ref[...]).astype(F32)
    row_ref[3 : 3 + attrs, :] = attr_ref[...]
    col_ref[...] = row_ref[...].T

    def project(j):
        at = span(j, 2 * TILE)
        value = nn(grid_ref[...], w_in_ref[:, at])
        high = value.astype(BF16)
        split_ref[pl.ds(0, grid_rows), at] = high
        split_ref[pl.ds(grid_rows, grid_rows), at] = (value - high.astype(F32)).astype(BF16)

    loop(c // (2 * TILE), project)

    def edge_forward(i):
        at = span(i, TILE)
        aux = col_ref[at, :]
        place = lax.broadcasted_iota(jnp.int32, (TILE, grid_rows), 1)
        table = (aux[:, 0:1].astype(jnp.int32) == place).astype(F32).astype(BF16)
        table = jnp.concatenate([table, table], axis=1)
        pre = nn(table, split_ref[...])
        for a in range(attrs):
            pre = pre + aux[:, 3 + a : 4 + a] * w_attr_ref[a : a + 1, :]
        sigma = 1.0 / (1.0 + jnp.exp(-pre))
        live = aux[:, 2:3]
        slope_ref[at, :] = sigma * (1.0 + pre * (1.0 - sigma)) * live
        hidden = (pre * sigma * live).astype(BF16)
        hid_ref[at, :] = hidden
        msg_ref[at, :] = nn(hidden, w_out_ref[...]).astype(BF16)

    for i in range(chunks):
        edge_forward(i)
        if i + 1 < n_mp:
            cot_hop(i + 1)
    for t in range(chunks + 1, n_mp):
        cot_hop(t)

    dest = dest_ref[...] - (me - 1) * nodes
    place = lax.broadcasted_iota(jnp.int32, (2 * nodes, edges), 0)
    place = jnp.where(place < nodes, place, place + nodes)
    sides = nn((dest == place).astype(F32).astype(BF16), msg_ref[...])
    hsend[0] = sides[:nodes].astype(BF16)
    hsend[1] = sides[nodes:].astype(BF16)
    down = copy(hsend.at[0], hrecv.at[1], halo_sem.at[0], along(-1))
    up = copy(hsend.at[1], hrecv.at[0], halo_sem.at[1], along(1))
    def exchange(lower, upper, low_slot, high_slot):
        @pl.when(jnp.logical_not(first))
        def _():
            lower.start()

        @pl.when(jnp.logical_not(last))
        def _():
            upper.start()

        @pl.when(first)
        def _():
            low_slot[...] = jnp.zeros_like(low_slot)

        @pl.when(last)
        def _():
            high_slot[...] = jnp.zeros_like(high_slot)

    def settle(lower, upper):
        @pl.when(jnp.logical_not(first))
        def _():
            lower.wait_send()
            upper.wait_recv()

        @pl.when(jnp.logical_not(last))
        def _():
            upper.wait_send()
            lower.wait_recv()

    exchange(down, up, hrecv.at[0], hrecv.at[1])
    place = lax.broadcasted_iota(jnp.int32, (nodes, edges), 0) + nodes
    node = mesh_ref[...].astype(F32) + nn(
        (dest == place).astype(F32).astype(BF16), msg_ref[...]
    )
    settle(down, up)
    node = node + hrecv[0].astype(F32) + hrecv[1].astype(F32)
    inv = lax.rsqrt(jnp.mean(node * node, axis=-1, keepdims=True) + EPS)
    node_ref[...] = node
    x_all[block(0), :] = (node * inv).astype(BF16)

    x_send, x_hop, x_drain = relay(x_all, x_sem)
    x_send(0)

    def qkv(o):
        band = x_all[block(o), :]
        for i in range(3):
            qkvg[i, block(o), :] = nn(band, w_qkv_ref[i]).astype(BF16)

    qkv(0)
    cot_drain()
    qkvg[3] = nt(cot_all[...], w_o_ref[...]).astype(BF16)

    def turn(j):
        at = span(j, TILE)
        hid_t[at, :] = hid_ref[:, at].T
        grid_t[at, :] = grid_ref[:, at].T

    loop(c // TILE, turn)
    for t in range(1, n_mp):
        x_hop(t, qkv)
    x_drain()

    lane = lax.broadcasted_iota(jnp.int32, (1, LANES), 1)

    def heads(p):
        at = span(p, LANES)
        q, k, v, g = (qkvg[i, :, at] for i in range(4))
        sums = [0.0] * 4
        for h in range(LANES // HDIM):
            own = jnp.logical_and(lane >= h * HDIM, lane < (h + 1) * HDIM)
            own = own.astype(F32).astype(BF16)
            qh, kh, vh, gh = q * own, k * own, v * own, g * own
            scores = nt(kh, q) * scale
            probs = jnp.exp(scores - jnp.max(scores, axis=0, keepdims=True))
            probs = probs * (1.0 / jnp.sum(probs, axis=0, keepdims=True))
            probs_b = probs.astype(BF16)
            dprob = nt(vh, g)
            delta = jnp.sum(probs * dprob, axis=0, keepdims=True)
            dscore = (probs * (dprob - delta) * scale).astype(BF16)
            sums[0] = sums[0] + tn(kh, dscore)
            sums[1] = sums[1] + nn(dscore, qh)
            sums[2] = sums[2] + nn(probs_b, gh)
            sums[3] = sums[3] + tn(vh, probs_b)
        dqkv[0, :, at] = sums[0].T.astype(BF16)
        dqkv[1, :, at] = sums[1].astype(BF16)
        dqkv[2, :, at] = sums[2].astype(BF16)
        att_ref[:, at] = sums[3].T.astype(BF16)

    loop(width // LANES, heads)

    value = nt(dqkv[0], w_qkv_ref[0])
    value = value + nt(dqkv[1], w_qkv_ref[1])
    value = value + nt(dqkv[2], w_qkv_ref[2])
    dxs[...] = value.astype(BF16)

    def right_sum(k):
        return copy(dxs.at[block(n_mp - k)], dxr.at[0, k - 1], dx_sem.at[0, k - 1], along(1))

    def left_sum(k):
        return copy(dxs.at[block(k)], dxr.at[1, k - 1], dx_sem.at[1, k - 1], along(-1))

    def pass_on(k):
        def add_in(way, slot):
            held = dxs[block(slot), :].astype(F32) + dxr[way, k].astype(F32)
            dxs[block(slot), :] = held.astype(BF16)

        @pl.when(me + k <= n_mp - 1)
        def _():
            if k < n_mp - 1:

                @pl.when(jnp.logical_not(first))
                def _():
                    right_sum(k + 1).wait_recv()
                    add_in(0, n_mp - k)

            right_sum(k).start()

        @pl.when(me >= k)
        def _():
            if k < n_mp - 1:

                @pl.when(jnp.logical_not(last))
                def _():
                    left_sum(k + 1).wait_recv()
                    add_in(1, k)

            left_sum(k).start()

    def keep(j):
        return (j * 2 + px) * (1 - core) + (py * 2 + j) * core

    def give(j):
        return (j * 2 + 1 - px) * (1 - core) + ((1 - py) * 2 + j) * core

    def stage(group, number):
        sems = rs_sem.at[group]
        mine = parts.at[group]
        if number == 0:
            return [copy(mine.at[1 - core], r1.at[group], sems.at[0], by_core)]
        if number == 1:
            return [
                copy(mine.at[core, give(j)], r2.at[group, j], sems.at[1 + j], second)
                for j in range(2)
            ]
        rest = (1 - py) * (1 - core) + (1 - px) * core
        return [copy(mine.at[core, keep(rest)], r3.at[group], sems.at[3], third)]

    def begin(group, number):
        for one in stage(group, number):
            one.start()

    def add(group, slot, other):
        value = parts[group, core, slot].astype(F32) + other.astype(F32)
        parts[group, core, slot] = value.astype(BF16)

    def finish_first(group):
        for one in stage(group, 0):
            one.wait()
        for j in range(2):
            add(group, give(j), r1[group, give(j)])
        begin(group, 1)
        for j in range(2):
            add(group, keep(j), r1[group, keep(j)])

    def finish_second(group):
        for one in stage(group, 1):
            one.wait()
        rest = (1 - py) * (1 - core) + (1 - px) * core
        add(group, keep(rest), r2[group, rest])
        begin(group, 2)
        add(group, keep(1 - rest), r2[group, 1 - rest])

    def finish_third(group):
        for one in stage(group, 2):
            one.wait()
        return parts[group, core, py * 2 + px].astype(F32) + r3[group].astype(F32)

    def pairs(fill):
        loop(parts.shape[2], fill)

    def fill_qkv(j):
        at = span(j, 2 * rows)
        x_part = x_all[:, at]
        for i in range(3):
            value = tn(x_part, dqkv[i]).astype(BF16)
            for side in range(2):
                parts[0, side, j, :, pl.ds(i * width, width)] = value[side * rows : (side + 1) * rows]
        value = tn(cot_all[:, at], att_ref[...]).astype(BF16)
        for side in range(2):
            parts[0, side, j, :, pl.ds(3 * width, width)] = value[side * rows : (side + 1) * rows]

    filled = parts.shape[2]
    for k in range(n_mp - 1, 0, -1):
        pass_on(k)
        if n_mp - 1 - k < filled:
            fill_qkv(n_mp - 1 - k)
    for j in range(n_mp - 1, filled):
        fill_qkv(j)
    begin(0, 0)

    for k in range(1, n_mp):

        @pl.when(me + k <= n_mp - 1)
        def _(k=k):
            right_sum(k).wait_send()

        @pl.when(me >= k)
        def _(k=k):
            left_sum(k).wait_send()

    @pl.when(first)
    def _():
        dxr[0, 0] = jnp.zeros_like(dxr[0, 0])

    @pl.when(last)
    def _():
        dxr[1, 0] = jnp.zeros_like(dxr[1, 0])

    @pl.when(jnp.logical_not(first))
    def _():
        right_sum(1).wait_recv()

    @pl.when(jnp.logical_not(last))
    def _():
        left_sum(1).wait_recv()

    dx = dxs[block(0), :].astype(F32) + dxr[0, 0].astype(F32) + dxr[1, 0].astype(F32)
    node = node_ref[...]
    inv = lax.rsqrt(jnp.mean(node * node, axis=-1, keepdims=True) + EPS)
    mean = jnp.mean(dx * node, axis=-1, keepdims=True)
    dnode = cot_ref[...].astype(F32) + inv * dx - node * inv * inv * inv * mean
    beside[pl.ds(nodes, nodes), :] = dnode.astype(BF16)
    middle = beside.at[pl.ds(nodes, nodes)]
    low, high = beside.at[pl.ds(0, nodes)], beside.at[pl.ds(2 * nodes, nodes)]
    down = copy(middle, high, beside_sem.at[0], along(-1))
    up = copy(middle, low, beside_sem.at[1], along(1))
    exchange(down, up, low, high)
    d_mesh_ref[...] = dnode.astype(BF16)
    finish_first(0)
    settle(down, up)

    def edge_gather(i):
        at = span(i, TILE)
        place = lax.broadcasted_iota(jnp.int32, (TILE, 3 * nodes), 1)
        aux = col_ref[at, :]
        table = (aux[:, 1:2].astype(jnp.int32) == place).astype(F32) * aux[:, 2:3]
        msg_ref[at, :] = nn(table.astype(BF16), beside[...]).astype(BF16)

    loop(chunks, edge_gather)

    def fill_out(j):
        value = nn(hid_t[span(j, 2 * rows), :], msg_ref[...]).astype(BF16)
        for side in range(2):
            parts[1, side, j] = value[side * rows : (side + 1) * rows]

    pairs(fill_out)
    begin(1, 0)
    finish_second(0)

    at_own[...] = jnp.zeros_like(at_own)

    def edge_backward(i):
        at = span(i, TILE)
        aux = col_ref[at, :]
        dpre = nt(msg_ref[at, :], w_out_ref[...]) * slope_ref[at, :]
        for a in range(attrs):
            at_own[a : a + 1, :] += jnp.sum(aux[:, 3 + a : 4 + a] * dpre, axis=0, keepdims=True)
        msg_ref[at, :] = dpre.astype(BF16)

    loop(chunks, edge_backward)
    finish_first(1)

    attr_steps = [
        copy(at_own, at_recv.at[i], at_sem.at[i], to) for i, to in enumerate((by_core, by_x, by_y))
    ]
    attr_steps[0].start()
    place = lax.broadcasted_iota(jnp.int32, (grid_rows, edges), 0)
    table = (source_ref[...] - me * grid_rows == place).astype(F32).astype(BF16)
    dproj_ref[...] = nn(table, msg_ref[...]).astype(BF16)

    def fill_in(j):
        value = nn(grid_t[span(j, 2 * rows), :], dproj_ref[...]).astype(BF16)
        for side in range(2):
            parts[2, side, j] = value[side * rows : (side + 1) * rows]

    pairs(fill_in)
    begin(2, 0)
    finish_second(1)
    attr_steps[0].wait()
    at_own[...] = at_own[...] + at_recv[0]
    attr_steps[1].start()

    def grid_back(j):
        at = span(j, 2 * TILE)
        d_grid_ref[:, at] = nt(dproj_ref[...], w_in_ref[at, :]).astype(BF16)

    finish_first(2)
    loop(c // (2 * TILE), grid_back)

    value = finish_third(0)
    for i in range(3):
        d_qkv_ref[i] = value[:, i * width : (i + 1) * width]
    d_o_ref[...] = value[:, 3 * width :].T
    attr_steps[1].wait()
    at_own[...] = at_own[...] + at_recv[1]
    attr_steps[2].start()

    def spread(group):
        value = finish_third(group)
        for t in range(n_mp):
            mpb[group - 1, t] = value[:, t * cols : (t + 1) * cols].astype(BF16)
        copies = [
            copy(
                mpb.at[group - 1, (me + o) % n_mp],
                mpr.at[group - 1, o - 1],
                mp_sem.at[group - 1, o - 1],
                along(o),
            )
            for o in range(1, n_mp)
        ]
        for one in copies:
            one.start()
        return copies

    def collect(group, copies, out_ref):
        for one in copies:
            one.wait()
        value = mpb[group - 1, me].astype(F32)
        for o in range(1, n_mp):
            value = value + mpr[group - 1, o - 1].astype(F32)
        out_ref[...] = value

    out_copies = spread(1)
    finish_second(2)
    attr_steps[2].wait()
    at_all[0] = at_own[...] + at_recv[2]
    attr_copies = [
        copy(at_all.at[0], at_all.at[o], at_sem.at[2 + o], along(o)) for o in range(1, n_mp)
    ]
    for one in attr_copies:
        one.start()
    in_copies = spread(2)
    for one in attr_copies:
        one.wait()
    value = at_all[me]
    for s in range(1, n_mp):
        value = value + at_all[(me + n_mp - s) % n_mp]
    d_attr_ref[...] = value
    collect(1, out_copies, d_out_ref)
    collect(2, in_copies, d_in_ref)


def write_out(*refs):
    sems = refs[-1]
    count = len(refs) // 2
    copies = [
        pltpu.make_async_copy(refs[i], refs[count + i], sems.at[i]) for i in range(count)
    ]
    for one in copies:
        one.start()
    for one in copies:
        one.wait()


def fused(
    grid_latent,
    mesh_latent,
    edge_source,
    edge_dest,
    edge_count,
    edge_attr,
    w_attr,
    w_in,
    w_out,
    w_qkv,
    w_o,
    cotangent,
):
    n_dp, n_mp = lax.axis_size("dp"), lax.axis_size("mp")
    grid_rows, c = grid_latent.shape[1:]
    nodes = mesh_latent.shape[1]
    edges = edge_source.shape[1]
    attrs = w_attr.shape[0]
    width = w_qkv.shape[2]
    total = nodes * n_mp
    rows, cols = c // n_dp, c // n_mp
    vmem = pl.BlockSpec(memory_space=pltpu.VMEM)
    shape = jax.ShapeDtypeStruct
    dma = pltpu.SemaphoreType.DMA
    outs = pl.pallas_call(
        functools.partial(layer_kernel, n_mp),
        out_shape=(
            shape((grid_rows, c), BF16),
            shape((nodes, c), BF16),
            shape((attrs, c), F32),
            shape((rows, cols), F32),
            shape((rows, cols), F32),
            shape((3, rows, width), F32),
            shape((width, rows), F32),
        ),
        in_specs=[vmem] * 12,
        out_specs=[vmem] * 7,
        scratch_shapes=[
            pltpu.VMEM((2 * grid_rows, c), BF16),
            pltpu.VMEM((edges, c), F32),
            pltpu.VMEM((edges, c), BF16),
            pltpu.VMEM((c, edges), BF16),
            pltpu.VMEM((c, grid_rows), BF16),
            pltpu.VMEM((edges, c), BF16),
            pltpu.VMEM(((attrs + 10) // 8 * 8, edges), F32),
            pltpu.VMEM((edges, (attrs + 10) // 8 * 8), F32),
            pltpu.VMEM((2, nodes, c), BF16),
            pltpu.VMEM((2, nodes, c), BF16),
            pltpu.VMEM((nodes, c), F32),
            pltpu.VMEM((total, c), BF16),
            pltpu.VMEM((total, c), BF16),
            pltpu.VMEM((4, total, width), BF16),
            pltpu.VMEM((3, total, width), BF16),
            pltpu.VMEM((total, width), BF16),
            pltpu.VMEM((total, c), BF16),
            pltpu.VMEM((2, n_mp - 1, nodes, c), BF16),
            pltpu.VMEM((3 * nodes, c), BF16),
            pltpu.VMEM((grid_rows, c), BF16),
            pltpu.VMEM((3, 2, n_dp // 2, rows, c), BF16),
            pltpu.VMEM((3, n_dp // 2, rows, c), BF16),
            pltpu.VMEM((3, 2, rows, c), BF16),
            pltpu.VMEM((3, rows, c), BF16),
            pltpu.VMEM((2, n_mp, rows, cols), BF16),
            pltpu.VMEM((2, n_mp - 1, rows, cols), BF16),
            pltpu.VMEM((attrs, c), F32),
            pltpu.VMEM((3, attrs, c), F32),
            pltpu.VMEM((n_mp, attrs, c), F32),
            dma((2, n_mp - 1, 2)),
            dma((2, n_mp - 1, 2)),
            dma((2, 2)),
            dma((2, n_mp - 1, 2)),
            dma((2, 2)),
            dma((3, 4, 2)),
            dma((2, n_mp - 1, 2)),
            dma((2 + n_mp, 2)),
        ],
        compiler_params=pltpu.CompilerParams(
            collective_id=0, has_side_effects=True, vmem_limit_bytes=58 * 2**20
        ),
    )(
        grid_latent[0],
        mesh_latent[0],
        edge_source,
        edge_dest,
        edge_count,
        edge_attr[0],
        w_attr,
        w_in,
        w_out,
        w_qkv,
        w_o,
        cotangent[0],
    )
    anywhere = pl.BlockSpec(memory_space=pl.ANY)
    outs = pl.pallas_call(
        write_out,
        out_shape=tuple(shape(one.shape, one.dtype) for one in outs),
        in_specs=[anywhere] * len(outs),
        out_specs=[anywhere] * len(outs),
        scratch_shapes=[dma((len(outs),))],
    )(*outs)
    return (outs[0][None], outs[1][None]) + tuple(outs[2:])


def step(*arrays):
    grid_latent, mesh_latent, edge_source, w_qkv = (arrays[i] for i in (0, 1, 2, 9))
    c, width = w_qkv.shape[1:]
    n_dp, n_mp = lax.axis_size("dp"), lax.axis_size("mp")
    fits = (
        n_dp == 8
        and n_mp % 2 == 0
        and n_mp * mesh_latent.shape[1] <= 512
        and 4 * width == c
        and width % LANES == 0
        and c % (2 * TILE) == 0
        and (c // n_dp) % LANES == 0
        and edge_source.shape[1] % TILE == 0
        and grid_latent.shape[1] % LANES == 0
    )
    return fused(*arrays) if fits else shards(*arrays)


def solution(mesh):
    return jax.shard_map(
        step,
        mesh=mesh,
        in_specs=(
            P("dp", "mp", None),
            P("dp", "mp", None),
            P("dp", "mp"),
            P("dp", "mp"),
            P("dp", "mp"),
            P("dp", None, "mp"),
            P(),
            P(),
            P(),
            P(None, None, "mp"),
            P("mp", None),
            P("dp", "mp", None),
        ),
        out_specs=(
            P("dp", "mp", None),
            P("dp", "mp", None),
            P(),
            P("dp", "mp"),
            P("dp", "mp"),
            P(None, "dp", "mp"),
            P("mp", "dp"),
        ),
        check_vma=False,
    )
```

```python
import functools

import jax
import jax.numpy as jnp
from jax import lax
from jax.experimental import pallas as pl
from jax.experimental.pallas import tpu as pltpu
from jax.sharding import PartitionSpec as P

HDIM = 64


EPS = 1e-06


def shifted(block, axis, distance):
    devices = range(lax.axis_size(axis))
    route = [(i - distance, i) for i in devices if i - distance in devices]
    return lax.ppermute(block, axis, route)


def with_halo(block, sides, width):
    for axis, dim in sides:
        count = lax.axis_size(axis)
        forward = [(i, i + 1) for i in range(count - 1)]
        backward = [(target, source) for source, target in forward]
        low = lax.ppermute(
            lax.slice_in_dim(block, block.shape[dim] - width, None, axis=dim), axis, forward
        )
        high = lax.ppermute(lax.slice_in_dim(block, 0, width, axis=dim), axis, backward)
        block = jnp.concatenate([low, block, high], axis=dim)
    return block


def shards(
    grid_latent,
    mesh_latent,
    edge_source,
    edge_dest,
    edge_count,
    edge_attr,
    w_attr,
    w_in,
    w_out,
    w_qkv,
    w_o,
    cotangent,
):
    band = lax.axis_index("mp")
    grid_rows = grid_latent.shape[1]
    nodes = mesh_latent.shape[1]
    edges = edge_source.shape[1]
    grid = grid_latent[0]
    live = (jnp.arange(edges, dtype=jnp.int32) < edge_count[0, 0]).astype(jnp.float32)[:, None]
    source_local = edge_source[0] - band * grid_rows
    dest_local = edge_dest[0] - (band - 1) * nodes
    projected = jnp.dot(grid, w_in, preferred_element_type=jnp.float32)
    attr_terms = lax.dot_general(
        edge_attr[0],
        w_attr,
        (((0,), (0,)), ((), ())),
        precision=lax.Precision.HIGHEST,
        preferred_element_type=jnp.float32,
    )
    preact = projected[source_local] + attr_terms
    hidden = (jax.nn.silu(preact) * live).astype(jnp.bfloat16)
    message = jnp.dot(hidden, w_out, preferred_element_type=jnp.float32).astype(jnp.bfloat16)
    dest_table = (dest_local[:, None] == jnp.arange(3 * nodes, dtype=jnp.int32)[None, :]).astype(
        jnp.bfloat16
    )
    partial_rows = lax.dot_general(
        dest_table, message, (((0,), (0,)), ((), ())), preferred_element_type=jnp.float32
    )
    from_below = shifted(partial_rows[2 * nodes :], "mp", 1)
    from_above = shifted(partial_rows[:nodes], "mp", -1)
    node = (
        mesh_latent[0].astype(jnp.float32)
        + partial_rows[nodes : 2 * nodes]
        + from_below
        + from_above
    )
    inv = lax.rsqrt(jnp.mean(node * node, axis=-1, keepdims=True) + EPS)
    normed = (node * inv).astype(jnp.bfloat16)
    all_normed, all_cot = (
        lax.all_gather(normed, "mp", axis=0, tiled=True),
        lax.all_gather(cotangent[0], "mp", axis=0, tiled=True),
    )
    total = all_normed.shape[0]
    width = w_qkv.shape[2]
    local_heads = width // HDIM
    qkv = jnp.einsum("nc,icd->ind", all_normed, w_qkv, preferred_element_type=jnp.float32).astype(
        jnp.bfloat16
    )
    qkv = qkv.reshape(3, total, local_heads, HDIM)
    query, keys, values = (qkv[0], qkv[1], qkv[2])
    d_att = lax.dot_general(
        all_cot, w_o, (((1,), (1,)), ((), ())), preferred_element_type=jnp.float32
    ).astype(jnp.bfloat16)
    d_att = d_att.reshape(total, local_heads, HDIM)
    block = min(512, total)
    scale = HDIM ** (-0.5)

    def attend_block(carry, index):
        key_acc, value_acc = carry
        start = index * block
        query_blk = lax.dynamic_slice_in_dim(query, start, block, 0)
        grad_blk = lax.dynamic_slice_in_dim(d_att, start, block, 0)
        scores = (
            jnp.einsum("qhd,khd->hqk", query_blk, keys, preferred_element_type=jnp.float32) * scale
        )
        probs = jax.nn.softmax(scores, axis=-1)
        probs_b = probs.astype(jnp.bfloat16)
        attended = jnp.einsum(
            "hqk,khd->qhd", probs_b, values, preferred_element_type=jnp.float32
        ).astype(jnp.bfloat16)
        dprob = jnp.einsum("qhd,khd->hqk", grad_blk, values, preferred_element_type=jnp.float32)
        delta = jnp.sum(probs * dprob, axis=-1, keepdims=True)
        dscore = (probs * (dprob - delta) * scale).astype(jnp.bfloat16)
        dquery = jnp.einsum(
            "hqk,khd->qhd", dscore, keys, preferred_element_type=jnp.float32
        ).astype(jnp.bfloat16)
        key_acc = key_acc + jnp.einsum(
            "hqk,qhd->khd", dscore, query_blk, preferred_element_type=jnp.float32
        )
        value_acc = value_acc + jnp.einsum(
            "hqk,qhd->khd", probs_b, grad_blk, preferred_element_type=jnp.float32
        )
        return ((key_acc, value_acc), (attended, dquery))

    empty = jnp.zeros((total, local_heads, HDIM), jnp.float32)
    sums, blocks = lax.scan(
        attend_block, (empty, empty), jnp.arange(total // block, dtype=jnp.int32)
    )
    attended = blocks[0].reshape(total, width)
    dquery = blocks[1].reshape(total, width)
    dkeys = sums[0].astype(jnp.bfloat16).reshape(total, width)
    dvalues = sums[1].astype(jnp.bfloat16).reshape(total, width)
    dqkv = jnp.stack([dquery, dkeys, dvalues])
    dw_o = lax.dot_general(
        attended, all_cot, (((0,), (0,)), ((), ())), preferred_element_type=jnp.float32
    )
    dw_qkv = jnp.einsum("nc,ind->icd", all_normed, dqkv, preferred_element_type=jnp.float32)
    sum_qkv, sum_o = (
        lax.psum_scatter(dw_qkv.astype(jnp.bfloat16), "dp", scatter_dimension=1, tiled=True).astype(
            jnp.float32
        ),
        lax.psum_scatter(dw_o.astype(jnp.bfloat16), "dp", scatter_dimension=1, tiled=True).astype(
            jnp.float32
        ),
    )
    dx = lax.psum_scatter(
        jnp.einsum("ind,icd->nc", dqkv, w_qkv, preferred_element_type=jnp.float32).astype(
            jnp.bfloat16
        ),
        "mp",
        scatter_dimension=0,
        tiled=True,
    ).astype(jnp.float32)
    dnode = (
        cotangent[0].astype(jnp.float32)
        + inv * dx
        - node * inv * inv * inv * jnp.mean(dx * node, axis=-1, keepdims=True)
    )
    d_mesh = dnode.astype(jnp.bfloat16)
    beside_all = with_halo(d_mesh, (("mp", 0),), nodes)
    dmessage = (beside_all[dest_local].astype(jnp.float32) * live).astype(jnp.bfloat16)
    dw_out = lax.dot_general(
        hidden, dmessage, (((0,), (0,)), ((), ())), preferred_element_type=jnp.float32
    )
    dhidden = lax.dot_general(
        dmessage, w_out, (((1,), (1,)), ((), ())), preferred_element_type=jnp.float32
    )
    sigma = jax.nn.sigmoid(preact)
    dpre = dhidden * sigma * (1.0 + preact * (1.0 - sigma)) * live
    dw_attr = jnp.dot(
        edge_attr[0], dpre, precision=lax.Precision.HIGHEST, preferred_element_type=jnp.float32
    )
    source_table = (
        source_local[:, None] == jnp.arange(grid_rows, dtype=jnp.int32)[None, :]
    ).astype(jnp.bfloat16)
    dproj = lax.dot_general(
        source_table,
        dpre.astype(jnp.bfloat16),
        (((0,), (0,)), ((), ())),
        preferred_element_type=jnp.float32,
    ).astype(jnp.bfloat16)
    dw_in = lax.dot_general(
        grid, dproj, (((0,), (0,)), ((), ())), preferred_element_type=jnp.float32
    )
    d_grid = lax.dot_general(
        dproj, w_in, (((1,), (1,)), ((), ())), preferred_element_type=jnp.float32
    ).astype(jnp.bfloat16)
    sum_attr = lax.psum(dw_attr, ("dp", "mp"))
    first_in, first_out = (
        lax.psum_scatter(dw_in.astype(jnp.bfloat16), "dp", scatter_dimension=0, tiled=True).astype(
            jnp.float32
        ),
        lax.psum_scatter(dw_out.astype(jnp.bfloat16), "dp", scatter_dimension=0, tiled=True).astype(
            jnp.float32
        ),
    )
    sum_in, sum_out = (
        lax.psum_scatter(
            first_in.astype(jnp.bfloat16), "mp", scatter_dimension=1, tiled=True
        ).astype(jnp.float32),
        lax.psum_scatter(
            first_out.astype(jnp.bfloat16), "mp", scatter_dimension=1, tiled=True
        ).astype(jnp.float32),
    )
    return (d_grid[None], d_mesh[None], sum_attr, sum_in, sum_out, sum_qkv, sum_o)


F32 = jnp.float32
BF16 = jnp.bfloat16
LANES = 128
TILE = 256


def nn(a, b):
    return jnp.dot(a, b, preferred_element_type=F32)


def nt(a, b):
    return lax.dot_general(a, b, (((1,), (1,)), ((), ())), preferred_element_type=F32)


def tn(a, b):
    return lax.dot_general(a, b, (((0,), (0,)), ((), ())), preferred_element_type=F32)


def span(index, size):
    return pl.ds(pl.multiple_of(index * size, size), size)


def loop(count, body):
    def step(i, carry):
        body(i)
        return carry

    lax.fori_loop(0, count, step, 0)


def layer_kernel(
    n_mp,
    grid_ref,
    mesh_ref,
    source_ref,
    dest_ref,
    count_ref,
    attr_ref,
    w_attr_ref,
    w_in_ref,
    w_out_hbm,
    w_qkv_hbm,
    w_o_hbm,
    cot_ref,
    d_grid_ref,
    d_mesh_ref,
    d_attr_ref,
    d_in_ref,
    d_out_ref,
    d_qkv_ref,
    d_o_ref,
    w_out_ref,
    w_qkv_ref,
    w_o_ref,
    split_ref,
    slope_ref,
    hid_ref,
    hid_t,
    grid_t,
    msg_ref,
    row_ref,
    col_ref,
    hsend,
    hrecv,
    node_ref,
    x_all,
    cot_all,
    qkvg,
    dqkv,
    att_ref,
    dxs,
    dxr,
    beside,
    dproj_ref,
    parts,
    r1,
    r2,
    r3,
    mpb,
    mpr,
    dpre_ref,
    at_own,
    at_recv,
    at_all,
    cot_sem,
    x_sem,
    halo_sem,
    dx_sem,
    beside_sem,
    rs_sem,
    mp_sem,
    at_sem,
    w_sem,
):
    d = lax.axis_index("dp")
    me = lax.axis_index("mp")
    core = d % 2
    px = (d // 2) % 2
    py = d // 4
    by_core = (d + 1 - 2 * core, me)
    by_x = (d + 2 - 4 * px, me)
    by_y = (d + 4 - 8 * py, me)
    second = (by_x[0] * (1 - core) + by_y[0] * core, me)
    third = (by_y[0] * (1 - core) + by_x[0] * core, me)

    def along(offset):
        return (d, (me + offset + n_mp) % n_mp)

    grid_rows, c = grid_ref.shape
    nodes = mesh_ref.shape[0]
    edges = source_ref.shape[1]
    attrs = w_attr_ref.shape[0]
    width = w_o_ref.shape[0]
    total = nodes * n_mp
    rows = parts.shape[3]
    cols = 2 * mpb.shape[3]
    scale = HDIM ** (-0.5)
    chunks = edges // TILE

    def copy(src, dst, sems, to):
        return pltpu.make_async_remote_copy(
            src_ref=src,
            dst_ref=dst,
            send_sem=sems.at[0],
            recv_sem=sems.at[1],
            device_id=to,
            device_id_type=pl.DeviceIdType.MESH,
        )

    loads = [
        pltpu.make_async_copy(w_out_hbm, w_out_ref, w_sem.at[0]),
        pltpu.make_async_copy(w_qkv_hbm, w_qkv_ref, w_sem.at[1]),
        pltpu.make_async_copy(w_o_hbm, w_o_ref, w_sem.at[2]),
    ]
    for one in loads:
        one.start()

    barrier = pltpu.get_barrier_semaphore()
    greeted = [by_core, by_x, by_y] + [along(o) for o in range(1, n_mp)]
    for other in greeted:
        pl.semaphore_signal(
            barrier, inc=1, device_id=other, device_id_type=pl.DeviceIdType.MESH
        )
    pl.semaphore_wait(barrier, len(greeted))

    def block(o):
        return pl.ds(o * nodes, nodes)

    first, last = me == 0, me == n_mp - 1

    def relay(blocks, sems):
        def right(t):
            return copy(blocks.at[block(t)], blocks.at[block(t + 1)], sems.at[0, t], along(1))

        def left(t):
            return copy(
                blocks.at[block((n_mp - t) % n_mp)],
                blocks.at[block(n_mp - t - 1)],
                sems.at[1, t],
                along(-1),
            )

        def send(t):
            @pl.when(jnp.logical_and(me >= t, jnp.logical_not(last)))
            def _():
                right(t).start()

            @pl.when(jnp.logical_and(me + t <= n_mp - 1, jnp.logical_not(first)))
            def _():
                left(t).start()

        def hop(t, use=None):
            @pl.when(me >= t)
            def _():
                right(t - 1).wait_recv()

            @pl.when(me + t <= n_mp - 1)
            def _():
                left(t - 1).wait_recv()

            if t < n_mp - 1:
                send(t)
            if use is not None:

                @pl.when(me >= t)
                def _():
                    use(t)

                @pl.when(me + t <= n_mp - 1)
                def _():
                    use(n_mp - t)

        def drain():
            for t in range(n_mp - 1):

                @pl.when(jnp.logical_and(me >= t, jnp.logical_not(last)))
                def _(t=t):
                    right(t).wait_send()

                @pl.when(jnp.logical_and(me + t <= n_mp - 1, jnp.logical_not(first)))
                def _(t=t):
                    left(t).wait_send()

        return send, hop, drain

    cot_all[block(0), :] = cot_ref[...]
    cot_send, cot_hop, cot_drain = relay(cot_all, cot_sem)
    cot_send(0)

    row_ref[...] = jnp.zeros_like(row_ref)
    row_ref[0:1, :] = (source_ref[...] - me * grid_rows).astype(F32)
    row_ref[1:2, :] = (dest_ref[...] - (me - 1) * nodes).astype(F32)
    position = lax.broadcasted_iota(jnp.int32, (1, edges), 1)
    row_ref[2:3, :] = (position < count_ref[...]).astype(F32)
    row_ref[3 : 3 + attrs, :] = attr_ref[...]
    col_ref[...] = row_ref[...].T

    def project(j):
        at = span(j, 2 * TILE)
        value = nn(grid_ref[...], w_in_ref[:, at])
        high = value.astype(BF16)
        split_ref[pl.ds(0, grid_rows), at] = high
        split_ref[pl.ds(grid_rows, grid_rows), at] = (value - high.astype(F32)).astype(BF16)

    loop(c // (2 * TILE), project)

    def edge_forward(i):
        at = span(i, TILE)
        aux = col_ref[at, :]
        place = lax.broadcasted_iota(jnp.int32, (TILE, grid_rows), 1)
        table = (aux[:, 0:1].astype(jnp.int32) == place).astype(F32).astype(BF16)
        table = jnp.concatenate([table, table], axis=1)
        pre = nn(table, split_ref[...])
        for a in range(attrs):
            pre = pre + aux[:, 3 + a : 4 + a] * w_attr_ref[a : a + 1, :]
        sigma = 1.0 / (1.0 + jnp.exp(-pre))
        live = aux[:, 2:3]
        slope_ref[at, :] = sigma * (1.0 + pre * (1.0 - sigma)) * live
        hidden = (pre * sigma * live).astype(BF16)
        hid_ref[at, :] = hidden
        msg_ref[at, :] = nn(hidden, w_out_ref[...]).astype(BF16)

    loads[0].wait()
    hops = 1
    for i in range(chunks):
        edge_forward(i)
        if hops < n_mp - 1:
            cot_hop(hops)
            hops = hops + 1

    dest = dest_ref[...] - (me - 1) * nodes
    place = lax.broadcasted_iota(jnp.int32, (2 * nodes, edges), 0)
    place = jnp.where(place < nodes, place, place + nodes)
    sides = nn((dest == place).astype(F32).astype(BF16), msg_ref[...])
    hsend[0] = sides[:nodes].astype(BF16)
    hsend[1] = sides[nodes:].astype(BF16)
    down = copy(hsend.at[0], hrecv.at[1], halo_sem.at[0], along(-1))
    up = copy(hsend.at[1], hrecv.at[0], halo_sem.at[1], along(1))
    def exchange(lower, upper, low_slot, high_slot):
        @pl.when(jnp.logical_not(first))
        def _():
            lower.start()

        @pl.when(jnp.logical_not(last))
        def _():
            upper.start()

        @pl.when(first)
        def _():
            low_slot[...] = jnp.zeros_like(low_slot)

        @pl.when(last)
        def _():
            high_slot[...] = jnp.zeros_like(high_slot)

    def settle(lower, upper):
        @pl.when(jnp.logical_not(first))
        def _():
            lower.wait_send()
            upper.wait_recv()

        @pl.when(jnp.logical_not(last))
        def _():
            upper.wait_send()
            lower.wait_recv()

    exchange(down, up, hrecv.at[0], hrecv.at[1])
    for t in range(hops, n_mp):
        cot_hop(t)
    place = lax.broadcasted_iota(jnp.int32, (nodes, edges), 0) + nodes
    node = mesh_ref[...].astype(F32) + nn(
        (dest == place).astype(F32).astype(BF16), msg_ref[...]
    )
    settle(down, up)
    node = node + hrecv[0].astype(F32) + hrecv[1].astype(F32)
    inv = lax.rsqrt(jnp.mean(node * node, axis=-1, keepdims=True) + EPS)
    node_ref[...] = node
    x_all[block(0), :] = (node * inv).astype(BF16)

    x_send, x_hop, x_drain = relay(x_all, x_sem)
    x_send(0)

    def qkv(o):
        band = x_all[block(o), :]
        for i in range(3):
            qkvg[i, block(o), :] = nn(band, w_qkv_ref[i]).astype(BF16)

    loads[1].wait()
    qkv(0)
    cot_drain()
    loads[2].wait()
    qkvg[3] = nt(cot_all[...], w_o_ref[...]).astype(BF16)

    def turn(j):
        at = span(j, TILE)
        hid_t[at, :] = hid_ref[:, at].T
        grid_t[at, :] = grid_ref[:, at].T

    loop(c // TILE, turn)
    for t in range(1, n_mp):
        x_hop(t, qkv)
    x_drain()

    lane = lax.broadcasted_iota(jnp.int32, (1, LANES), 1)

    def heads(p):
        at = span(p, LANES)
        q, k, v, g = (qkvg[i, :, at] for i in range(4))
        sums = [0.0] * 4
        for h in range(LANES // HDIM):
            own = jnp.logical_and(lane >= h * HDIM, lane < (h + 1) * HDIM)
            own = own.astype(F32).astype(BF16)
            qh, kh, vh, gh = q * own, k * own, v * own, g * own
            scores = nt(kh, q) * scale
            probs = jnp.exp(scores - jnp.max(scores, axis=0, keepdims=True))
            probs = probs * (1.0 / jnp.sum(probs, axis=0, keepdims=True))
            probs_b = probs.astype(BF16)
            dprob = nt(vh, g)
            delta = jnp.sum(probs * dprob, axis=0, keepdims=True)
            dscore = (probs * (dprob - delta) * scale).astype(BF16)
            sums[0] = sums[0] + tn(kh, dscore)
            sums[1] = sums[1] + nn(dscore, qh)
            sums[2] = sums[2] + nn(probs_b, gh)
            sums[3] = sums[3] + tn(vh, probs_b)
        dqkv[0, :, at] = sums[0].T.astype(BF16)
        dqkv[1, :, at] = sums[1].astype(BF16)
        dqkv[2, :, at] = sums[2].astype(BF16)
        att_ref[:, at] = sums[3].T.astype(BF16)

    loop(width // LANES, heads)

    value = nt(dqkv[0], w_qkv_ref[0])
    value = value + nt(dqkv[1], w_qkv_ref[1])
    value = value + nt(dqkv[2], w_qkv_ref[2])
    dxs[...] = value.astype(BF16)

    def right_sum(k):
        return copy(dxs.at[block(n_mp - k)], dxr.at[0, k - 1], dx_sem.at[0, k - 1], along(1))

    def left_sum(k):
        return copy(dxs.at[block(k)], dxr.at[1, k - 1], dx_sem.at[1, k - 1], along(-1))

    def pass_on(k):
        def add_in(way, slot):
            held = dxs[block(slot), :].astype(F32) + dxr[way, k].astype(F32)
            dxs[block(slot), :] = held.astype(BF16)

        @pl.when(me + k <= n_mp - 1)
        def _():
            if k < n_mp - 1:

                @pl.when(jnp.logical_not(first))
                def _():
                    right_sum(k + 1).wait_recv()
                    add_in(0, n_mp - k)

            right_sum(k).start()

        @pl.when(me >= k)
        def _():
            if k < n_mp - 1:

                @pl.when(jnp.logical_not(last))
                def _():
                    left_sum(k + 1).wait_recv()
                    add_in(1, k)

            left_sum(k).start()

    def keep(j):
        return (j * 2 + px) * (1 - core) + (py * 2 + j) * core

    def give(j):
        return (j * 2 + 1 - px) * (1 - core) + ((1 - py) * 2 + j) * core

    def stage(group, number):
        sems = rs_sem.at[group]
        mine = parts.at[group]
        if number == 0:
            return [copy(mine.at[1 - core], r1.at[group], sems.at[0], by_core)]
        if number == 1:
            return [
                copy(mine.at[core, give(j)], r2.at[group, j], sems.at[1 + j], second)
                for j in range(2)
            ]
        rest = (1 - py) * (1 - core) + (1 - px) * core
        return [copy(mine.at[core, keep(rest)], r3.at[group], sems.at[3], third)]

    def begin(group, number):
        for one in stage(group, number):
            one.start()

    def add(group, slot, other):
        value = parts[group, core, slot].astype(F32) + other.astype(F32)
        parts[group, core, slot] = value.astype(BF16)

    def finish_first(group):
        for one in stage(group, 0):
            one.wait()
        for j in range(2):
            add(group, give(j), r1[group, give(j)])
        begin(group, 1)
        for j in range(2):
            add(group, keep(j), r1[group, keep(j)])

    def finish_second(group):
        for one in stage(group, 1):
            one.wait()
        rest = (1 - py) * (1 - core) + (1 - px) * core
        add(group, keep(rest), r2[group, rest])
        begin(group, 2)
        add(group, keep(1 - rest), r2[group, 1 - rest])

    def finish_third(group):
        for one in stage(group, 2):
            one.wait()
        return parts[group, core, py * 2 + px].astype(F32) + r3[group].astype(F32)

    def put(group, j, value, start=0):
        value = value.astype(BF16)
        for side in range(2):
            parts[group, side, j, :, start : start + value.shape[1]] = value[
                side * rows : (side + 1) * rows
            ]

    def pairs(group, fill):
        loop(parts.shape[2], fill)
        begin(group, 0)

    def fill_qk(j):
        x_part = x_all[:, span(j, 2 * rows)]
        for i in range(2):
            put(0, j, tn(x_part, dqkv[i]), i * width)

    def fill_vo(j):
        at = span(j, 2 * rows)
        put(1, j, tn(x_all[:, at], dqkv[2]))
        put(1, j, tn(cot_all[:, at], att_ref[...]), width)

    fills = [functools.partial(pairs, 0, fill_qk), functools.partial(pairs, 1, fill_vo)]
    for k in range(n_mp - 1, 0, -1):
        pass_on(k)
        if fills:
            fills.pop(0)()
    for fill in fills:
        fill()
    finish_first(0)

    for k in range(1, n_mp):

        @pl.when(me + k <= n_mp - 1)
        def _(k=k):
            right_sum(k).wait_send()

        @pl.when(me >= k)
        def _(k=k):
            left_sum(k).wait_send()

    @pl.when(first)
    def _():
        dxr[0, 0] = jnp.zeros_like(dxr[0, 0])

    @pl.when(last)
    def _():
        dxr[1, 0] = jnp.zeros_like(dxr[1, 0])

    @pl.when(jnp.logical_not(first))
    def _():
        right_sum(1).wait_recv()

    @pl.when(jnp.logical_not(last))
    def _():
        left_sum(1).wait_recv()

    dx = dxs[block(0), :].astype(F32) + dxr[0, 0].astype(F32) + dxr[1, 0].astype(F32)
    node = node_ref[...]
    inv = lax.rsqrt(jnp.mean(node * node, axis=-1, keepdims=True) + EPS)
    mean = jnp.mean(dx * node, axis=-1, keepdims=True)
    dnode = cot_ref[...].astype(F32) + inv * dx - node * inv * inv * inv * mean
    beside[pl.ds(nodes, nodes), :] = dnode.astype(BF16)
    middle = beside.at[pl.ds(nodes, nodes)]
    low, high = beside.at[pl.ds(0, nodes)], beside.at[pl.ds(2 * nodes, nodes)]
    down = copy(middle, high, beside_sem.at[0], along(-1))
    up = copy(middle, low, beside_sem.at[1], along(1))
    exchange(down, up, low, high)
    d_mesh_ref[...] = dnode.astype(BF16)
    finish_first(1)
    settle(down, up)

    def edge_gather(i):
        at = span(i, TILE)
        place = lax.broadcasted_iota(jnp.int32, (TILE, 3 * nodes), 1)
        aux = col_ref[at, :]
        table = (aux[:, 1:2].astype(jnp.int32) == place).astype(F32) * aux[:, 2:3]
        msg_ref[at, :] = nn(table.astype(BF16), beside[...]).astype(BF16)

    loop(chunks, edge_gather)

    half = cols // 2

    def pieces(h):
        return [pl.ds(t * cols + h * half, half) for t in range(n_mp)]

    def columns(ref, at, h):
        return jnp.concatenate([ref[at, piece] for piece in pieces(h)], axis=1)

    def grad_out(h):
        def fill(j):
            put(2 + h, j, nn(hid_t[span(j, 2 * rows), :], columns(msg_ref, pl.ds(0, edges), h)))

        pairs(2 + h, fill)

    grad_out(0)
    finish_second(0)
    grad_out(1)
    finish_second(1)
    finish_first(2)

    at_own[...] = jnp.zeros_like(at_own)
    place = lax.broadcasted_iota(jnp.int32, (grid_rows, edges), 0)
    source_table = (source_ref[...] - me * grid_rows == place).astype(F32).astype(BF16)

    def grad_in(h):
        def edge_backward(i):
            at = span(i, TILE)
            aux = col_ref[at, :]
            weight = jnp.concatenate([w_out_ref[piece, :] for piece in pieces(h)], axis=0)
            dpre = nt(msg_ref[at, :], weight) * columns(slope_ref, at, h)
            for a in range(attrs):
                value = jnp.sum(aux[:, 3 + a : 4 + a] * dpre, axis=0, keepdims=True)
                for t, piece in enumerate(pieces(h)):
                    at_own[a : a + 1, piece] += value[:, t * half : (t + 1) * half]
            dpre_ref[at, :] = dpre.astype(BF16)

        loop(chunks, edge_backward)
        dproj = nn(source_table, dpre_ref[...]).astype(BF16)
        for t, piece in enumerate(pieces(h)):
            dproj_ref[:, piece] = dproj[:, t * half : (t + 1) * half]

        def fill(j):
            put(4 + h, j, nn(grid_t[span(j, 2 * rows), :], columns(dproj_ref, pl.ds(0, grid_rows), h)))

        pairs(4 + h, fill)

    grad_in(0)
    finish_first(3)
    finish_second(2)
    grad_in(1)
    finish_first(4)
    finish_second(3)

    attr_steps = [
        copy(at_own, at_recv.at[i], at_sem.at[i], to) for i, to in enumerate((by_core, by_x, by_y))
    ]
    attr_steps[0].start()

    def grid_back(j):
        at = span(j, 2 * TILE)
        d_grid_ref[:, at] = nt(dproj_ref[...], w_in_ref[at, :]).astype(BF16)

    finish_first(5)
    loop(c // (2 * TILE), grid_back)
    attr_steps[0].wait()
    at_own[...] = at_own[...] + at_recv[0]
    attr_steps[1].start()
    value = finish_third(0)
    for i in range(2):
        d_qkv_ref[i] = value[:, i * width : (i + 1) * width]
    value = finish_third(1)
    d_qkv_ref[2] = value[:, :width]
    d_o_ref[...] = value[:, width:].T

    def spread(group):
        slot = group - 2
        value = finish_third(group)
        for t in range(n_mp):
            mpb[slot, t] = value[:, t * half : (t + 1) * half].astype(BF16)
        copies = [
            copy(mpb.at[slot, (me + o) % n_mp], mpr.at[slot, o - 1], mp_sem.at[slot, o - 1], along(o))
            for o in range(1, n_mp)
        ]
        for one in copies:
            one.start()
        return copies

    def collect(group, copies, out_ref, h):
        slot = group - 2
        for one in copies:
            one.wait()
        value = mpb[slot, me].astype(F32)
        for o in range(1, n_mp):
            value = value + mpr[slot, o - 1].astype(F32)
        out_ref[:, h * half : (h + 1) * half] = value

    copies = [spread(2)]
    finish_second(4)
    copies.append(spread(3))
    attr_steps[1].wait()
    at_own[...] = at_own[...] + at_recv[1]
    attr_steps[2].start()
    finish_second(5)
    copies.append(spread(4))
    attr_steps[2].wait()
    at_all[0] = at_own[...] + at_recv[2]
    attr_copies = [
        copy(at_all.at[0], at_all.at[o], at_sem.at[2 + o], along(o)) for o in range(1, n_mp)
    ]
    for one in attr_copies:
        one.start()
    copies.append(spread(5))
    collect(2, copies[0], d_out_ref, 0)
    collect(3, copies[1], d_out_ref, 1)
    for one in attr_copies:
        one.wait()
    value = at_all[me]
    for s in range(1, n_mp):
        value = value + at_all[(me + n_mp - s) % n_mp]
    d_attr_ref[...] = value
    collect(4, copies[2], d_in_ref, 0)
    collect(5, copies[3], d_in_ref, 1)


def write_out(*refs):
    sems = refs[-1]
    count = len(refs) // 2
    copies = [
        pltpu.make_async_copy(refs[i], refs[count + i], sems.at[i]) for i in range(count)
    ]
    for one in copies:
        one.start()
    for one in copies:
        one.wait()


def fused(
    grid_latent,
    mesh_latent,
    edge_source,
    edge_dest,
    edge_count,
    edge_attr,
    w_attr,
    w_in,
    w_out,
    w_qkv,
    w_o,
    cotangent,
):
    n_dp, n_mp = lax.axis_size("dp"), lax.axis_size("mp")
    grid_rows, c = grid_latent.shape[1:]
    nodes = mesh_latent.shape[1]
    edges = edge_source.shape[1]
    attrs = w_attr.shape[0]
    width = w_qkv.shape[2]
    total = nodes * n_mp
    rows, cols = c // n_dp, c // n_mp
    vmem = pl.BlockSpec(memory_space=pltpu.VMEM)
    anywhere = pl.BlockSpec(memory_space=pl.ANY)
    shape = jax.ShapeDtypeStruct
    dma = pltpu.SemaphoreType.DMA
    outs = pl.pallas_call(
        functools.partial(layer_kernel, n_mp),
        out_shape=(
            shape((grid_rows, c), BF16),
            shape((nodes, c), BF16),
            shape((attrs, c), F32),
            shape((rows, cols), F32),
            shape((rows, cols), F32),
            shape((3, rows, width), F32),
            shape((width, rows), F32),
        ),
        in_specs=[vmem] * 8 + [anywhere] * 3 + [vmem],
        out_specs=[vmem] * 7,
        scratch_shapes=[
            pltpu.VMEM(w_out.shape, BF16),
            pltpu.VMEM(w_qkv.shape, BF16),
            pltpu.VMEM(w_o.shape, BF16),
            pltpu.VMEM((2 * grid_rows, c), BF16),
            pltpu.VMEM((edges, c), F32),
            pltpu.VMEM((edges, c), BF16),
            pltpu.VMEM((c, edges), BF16),
            pltpu.VMEM((c, grid_rows), BF16),
            pltpu.VMEM((edges, c), BF16),
            pltpu.VMEM(((attrs + 10) // 8 * 8, edges), F32),
            pltpu.VMEM((edges, (attrs + 10) // 8 * 8), F32),
            pltpu.VMEM((2, nodes, c), BF16),
            pltpu.VMEM((2, nodes, c), BF16),
            pltpu.VMEM((nodes, c), F32),
            pltpu.VMEM((total, c), BF16),
            pltpu.VMEM((total, c), BF16),
            pltpu.VMEM((4, total, width), BF16),
            pltpu.VMEM((3, total, width), BF16),
            pltpu.VMEM((total, width), BF16),
            pltpu.VMEM((total, c), BF16),
            pltpu.VMEM((2, n_mp - 1, nodes, c), BF16),
            pltpu.VMEM((3 * nodes, c), BF16),
            pltpu.VMEM((grid_rows, c), BF16),
            pltpu.VMEM((6, 2, n_dp // 2, rows, c // 2), BF16),
            pltpu.VMEM((6, n_dp // 2, rows, c // 2), BF16),
            pltpu.VMEM((6, 2, rows, c // 2), BF16),
            pltpu.VMEM((6, rows, c // 2), BF16),
            pltpu.VMEM((4, n_mp, rows, cols // 2), BF16),
            pltpu.VMEM((4, n_mp - 1, rows, cols // 2), BF16),
            pltpu.VMEM((edges, c // 2), BF16),
            pltpu.VMEM((attrs, c), F32),
            pltpu.VMEM((3, attrs, c), F32),
            pltpu.VMEM((n_mp, attrs, c), F32),
            dma((2, n_mp - 1, 2)),
            dma((2, n_mp - 1, 2)),
            dma((2, 2)),
            dma((2, n_mp - 1, 2)),
            dma((2, 2)),
            dma((6, 4, 2)),
            dma((4, n_mp - 1, 2)),
            dma((2 + n_mp, 2)),
            dma((3,)),
        ],
        compiler_params=pltpu.CompilerParams(
            collective_id=0, has_side_effects=True, vmem_limit_bytes=58 * 2**20
        ),
    )(
        grid_latent[0],
        mesh_latent[0],
        edge_source,
        edge_dest,
        edge_count,
        edge_attr[0],
        w_attr,
        w_in,
        w_out,
        w_qkv,
        w_o,
        cotangent[0],
    )
    outs = pl.pallas_call(
        write_out,
        out_shape=tuple(shape(one.shape, one.dtype) for one in outs),
        in_specs=[vmem] * len(outs),
        out_specs=[anywhere] * len(outs),
        scratch_shapes=[dma((len(outs),))],
    )(*outs)
    return (outs[0][None], outs[1][None]) + tuple(outs[2:])


def step(*arrays):
    grid_latent, mesh_latent, edge_source, w_qkv = (arrays[i] for i in (0, 1, 2, 9))
    c, width = w_qkv.shape[1:]
    n_dp, n_mp = lax.axis_size("dp"), lax.axis_size("mp")
    fits = (
        n_dp == 8
        and n_mp % 2 == 0
        and n_mp * mesh_latent.shape[1] <= 512
        and 4 * width == c
        and width % (2 * LANES) == 0
        and c % (2 * TILE) == 0
        and (c // n_dp) % LANES == 0
        and edge_source.shape[1] % TILE == 0
        and grid_latent.shape[1] % LANES == 0
    )
    return fused(*arrays) if fits else shards(*arrays)


def solution(mesh):
    return jax.shard_map(
        step,
        mesh=mesh,
        in_specs=(
            P("dp", "mp", None),
            P("dp", "mp", None),
            P("dp", "mp"),
            P("dp", "mp"),
            P("dp", "mp"),
            P("dp", None, "mp"),
            P(),
            P(),
            P(),
            P(None, None, "mp"),
            P("mp", None),
            P("dp", "mp", None),
        ),
        out_specs=(
            P("dp", "mp", None),
            P("dp", "mp", None),
            P(),
            P("dp", "mp"),
            P("dp", "mp"),
            P(None, "dp", "mp"),
            P("mp", "dp"),
        ),
        check_vma=False,
    )
```

```python
import functools

import jax
import jax.numpy as jnp
from jax import lax
from jax.experimental import pallas as pl
from jax.experimental.pallas import tpu as pltpu
from jax.sharding import PartitionSpec as P

HDIM = 64


EPS = 1e-06


def shifted(block, axis, distance):
    devices = range(lax.axis_size(axis))
    route = [(i - distance, i) for i in devices if i - distance in devices]
    return lax.ppermute(block, axis, route)


def with_halo(block, sides, width):
    for axis, dim in sides:
        count = lax.axis_size(axis)
        forward = [(i, i + 1) for i in range(count - 1)]
        backward = [(target, source) for source, target in forward]
        low = lax.ppermute(
            lax.slice_in_dim(block, block.shape[dim] - width, None, axis=dim), axis, forward
        )
        high = lax.ppermute(lax.slice_in_dim(block, 0, width, axis=dim), axis, backward)
        block = jnp.concatenate([low, block, high], axis=dim)
    return block


def shards(
    grid_latent,
    mesh_latent,
    edge_source,
    edge_dest,
    edge_count,
    edge_attr,
    w_attr,
    w_in,
    w_out,
    w_qkv,
    w_o,
    cotangent,
):
    band = lax.axis_index("mp")
    grid_rows = grid_latent.shape[1]
    nodes = mesh_latent.shape[1]
    edges = edge_source.shape[1]
    grid = grid_latent[0]
    live = (jnp.arange(edges, dtype=jnp.int32) < edge_count[0, 0]).astype(jnp.float32)[:, None]
    source_local = edge_source[0] - band * grid_rows
    dest_local = edge_dest[0] - (band - 1) * nodes
    projected = jnp.dot(grid, w_in, preferred_element_type=jnp.float32)
    attr_terms = lax.dot_general(
        edge_attr[0],
        w_attr,
        (((0,), (0,)), ((), ())),
        precision=lax.Precision.HIGHEST,
        preferred_element_type=jnp.float32,
    )
    preact = projected[source_local] + attr_terms
    hidden = (jax.nn.silu(preact) * live).astype(jnp.bfloat16)
    message = jnp.dot(hidden, w_out, preferred_element_type=jnp.float32).astype(jnp.bfloat16)
    dest_table = (dest_local[:, None] == jnp.arange(3 * nodes, dtype=jnp.int32)[None, :]).astype(
        jnp.bfloat16
    )
    partial_rows = lax.dot_general(
        dest_table, message, (((0,), (0,)), ((), ())), preferred_element_type=jnp.float32
    )
    from_below = shifted(partial_rows[2 * nodes :], "mp", 1)
    from_above = shifted(partial_rows[:nodes], "mp", -1)
    node = (
        mesh_latent[0].astype(jnp.float32)
        + partial_rows[nodes : 2 * nodes]
        + from_below
        + from_above
    )
    inv = lax.rsqrt(jnp.mean(node * node, axis=-1, keepdims=True) + EPS)
    normed = (node * inv).astype(jnp.bfloat16)
    all_normed, all_cot = (
        lax.all_gather(normed, "mp", axis=0, tiled=True),
        lax.all_gather(cotangent[0], "mp", axis=0, tiled=True),
    )
    total = all_normed.shape[0]
    width = w_qkv.shape[2]
    local_heads = width // HDIM
    qkv = jnp.einsum("nc,icd->ind", all_normed, w_qkv, preferred_element_type=jnp.float32).astype(
        jnp.bfloat16
    )
    qkv = qkv.reshape(3, total, local_heads, HDIM)
    query, keys, values = (qkv[0], qkv[1], qkv[2])
    d_att = lax.dot_general(
        all_cot, w_o, (((1,), (1,)), ((), ())), preferred_element_type=jnp.float32
    ).astype(jnp.bfloat16)
    d_att = d_att.reshape(total, local_heads, HDIM)
    block = min(512, total)
    scale = HDIM ** (-0.5)

    def attend_block(carry, index):
        key_acc, value_acc = carry
        start = index * block
        query_blk = lax.dynamic_slice_in_dim(query, start, block, 0)
        grad_blk = lax.dynamic_slice_in_dim(d_att, start, block, 0)
        scores = (
            jnp.einsum("qhd,khd->hqk", query_blk, keys, preferred_element_type=jnp.float32) * scale
        )
        probs = jax.nn.softmax(scores, axis=-1)
        probs_b = probs.astype(jnp.bfloat16)
        attended = jnp.einsum(
            "hqk,khd->qhd", probs_b, values, preferred_element_type=jnp.float32
        ).astype(jnp.bfloat16)
        dprob = jnp.einsum("qhd,khd->hqk", grad_blk, values, preferred_element_type=jnp.float32)
        delta = jnp.sum(probs * dprob, axis=-1, keepdims=True)
        dscore = (probs * (dprob - delta) * scale).astype(jnp.bfloat16)
        dquery = jnp.einsum(
            "hqk,khd->qhd", dscore, keys, preferred_element_type=jnp.float32
        ).astype(jnp.bfloat16)
        key_acc = key_acc + jnp.einsum(
            "hqk,qhd->khd", dscore, query_blk, preferred_element_type=jnp.float32
        )
        value_acc = value_acc + jnp.einsum(
            "hqk,qhd->khd", probs_b, grad_blk, preferred_element_type=jnp.float32
        )
        return ((key_acc, value_acc), (attended, dquery))

    empty = jnp.zeros((total, local_heads, HDIM), jnp.float32)
    sums, blocks = lax.scan(
        attend_block, (empty, empty), jnp.arange(total // block, dtype=jnp.int32)
    )
    attended = blocks[0].reshape(total, width)
    dquery = blocks[1].reshape(total, width)
    dkeys = sums[0].astype(jnp.bfloat16).reshape(total, width)
    dvalues = sums[1].astype(jnp.bfloat16).reshape(total, width)
    dqkv = jnp.stack([dquery, dkeys, dvalues])
    dw_o = lax.dot_general(
        attended, all_cot, (((0,), (0,)), ((), ())), preferred_element_type=jnp.float32
    )
    dw_qkv = jnp.einsum("nc,ind->icd", all_normed, dqkv, preferred_element_type=jnp.float32)
    sum_qkv, sum_o = (
        lax.psum_scatter(dw_qkv.astype(jnp.bfloat16), "dp", scatter_dimension=1, tiled=True).astype(
            jnp.float32
        ),
        lax.psum_scatter(dw_o.astype(jnp.bfloat16), "dp", scatter_dimension=1, tiled=True).astype(
            jnp.float32
        ),
    )
    dx = lax.psum_scatter(
        jnp.einsum("ind,icd->nc", dqkv, w_qkv, preferred_element_type=jnp.float32).astype(
            jnp.bfloat16
        ),
        "mp",
        scatter_dimension=0,
        tiled=True,
    ).astype(jnp.float32)
    dnode = (
        cotangent[0].astype(jnp.float32)
        + inv * dx
        - node * inv * inv * inv * jnp.mean(dx * node, axis=-1, keepdims=True)
    )
    d_mesh = dnode.astype(jnp.bfloat16)
    beside_all = with_halo(d_mesh, (("mp", 0),), nodes)
    dmessage = (beside_all[dest_local].astype(jnp.float32) * live).astype(jnp.bfloat16)
    dw_out = lax.dot_general(
        hidden, dmessage, (((0,), (0,)), ((), ())), preferred_element_type=jnp.float32
    )
    dhidden = lax.dot_general(
        dmessage, w_out, (((1,), (1,)), ((), ())), preferred_element_type=jnp.float32
    )
    sigma = jax.nn.sigmoid(preact)
    dpre = dhidden * sigma * (1.0 + preact * (1.0 - sigma)) * live
    dw_attr = jnp.dot(
        edge_attr[0], dpre, precision=lax.Precision.HIGHEST, preferred_element_type=jnp.float32
    )
    source_table = (
        source_local[:, None] == jnp.arange(grid_rows, dtype=jnp.int32)[None, :]
    ).astype(jnp.bfloat16)
    dproj = lax.dot_general(
        source_table,
        dpre.astype(jnp.bfloat16),
        (((0,), (0,)), ((), ())),
        preferred_element_type=jnp.float32,
    ).astype(jnp.bfloat16)
    dw_in = lax.dot_general(
        grid, dproj, (((0,), (0,)), ((), ())), preferred_element_type=jnp.float32
    )
    d_grid = lax.dot_general(
        dproj, w_in, (((1,), (1,)), ((), ())), preferred_element_type=jnp.float32
    ).astype(jnp.bfloat16)
    sum_attr = lax.psum(dw_attr, ("dp", "mp"))
    first_in, first_out = (
        lax.psum_scatter(dw_in.astype(jnp.bfloat16), "dp", scatter_dimension=0, tiled=True).astype(
            jnp.float32
        ),
        lax.psum_scatter(dw_out.astype(jnp.bfloat16), "dp", scatter_dimension=0, tiled=True).astype(
            jnp.float32
        ),
    )
    sum_in, sum_out = (
        lax.psum_scatter(
            first_in.astype(jnp.bfloat16), "mp", scatter_dimension=1, tiled=True
        ).astype(jnp.float32),
        lax.psum_scatter(
            first_out.astype(jnp.bfloat16), "mp", scatter_dimension=1, tiled=True
        ).astype(jnp.float32),
    )
    return (d_grid[None], d_mesh[None], sum_attr, sum_in, sum_out, sum_qkv, sum_o)


F32 = jnp.float32
BF16 = jnp.bfloat16
LANES = 128
TILE = 256


def nn(a, b):
    return jnp.dot(a, b, preferred_element_type=F32)


def nt(a, b):
    return lax.dot_general(a, b, (((1,), (1,)), ((), ())), preferred_element_type=F32)


def tn(a, b):
    return lax.dot_general(a, b, (((0,), (0,)), ((), ())), preferred_element_type=F32)


def span(index, size):
    return pl.ds(pl.multiple_of(index * size, size), size)


def loop(count, body):
    def step(i, carry):
        body(i)
        return carry

    lax.fori_loop(0, count, step, 0)


def layer_kernel(
    n_mp,
    grid_ref,
    mesh_ref,
    source_ref,
    dest_ref,
    count_ref,
    attr_ref,
    w_attr_ref,
    w_in_ref,
    w_out_hbm,
    w_qkv_hbm,
    w_o_hbm,
    cot_ref,
    d_grid_ref,
    d_mesh_ref,
    d_attr_ref,
    d_in_ref,
    d_out_ref,
    d_qkv_ref,
    d_o_ref,
    w_out_ref,
    w_qkv_ref,
    w_o_ref,
    split_ref,
    slope_ref,
    hid_ref,
    hid_t,
    grid_t,
    msg_ref,
    row_ref,
    col_ref,
    hsend,
    hrecv,
    node_ref,
    x_all,
    cot_all,
    qkvg,
    dqkv,
    att_ref,
    dxs,
    dxr,
    beside,
    dproj_ref,
    parts,
    r1,
    r2,
    r3,
    mpb,
    mpr,
    dpre_ref,
    table_ref,
    dest_table_ref,
    gather_ref,
    source_table,
    at_own,
    at_recv,
    at_all,
    cot_sem,
    x_sem,
    halo_sem,
    dx_sem,
    beside_sem,
    rs_sem,
    mp_sem,
    at_sem,
    w_sem,
):
    d = lax.axis_index("dp")
    me = lax.axis_index("mp")
    core = d % 2
    px = (d // 2) % 2
    py = d // 4
    by_core = (d + 1 - 2 * core, me)
    by_x = (d + 2 - 4 * px, me)
    by_y = (d + 4 - 8 * py, me)
    second = (by_x[0] * (1 - core) + by_y[0] * core, me)
    third = (by_y[0] * (1 - core) + by_x[0] * core, me)

    def along(offset):
        return (d, (me + offset + n_mp) % n_mp)

    grid_rows, c = grid_ref.shape
    nodes = mesh_ref.shape[0]
    edges = source_ref.shape[1]
    attrs = w_attr_ref.shape[0]
    width = w_o_ref.shape[0]
    total = nodes * n_mp
    rows = parts.shape[3]
    cols = 2 * mpb.shape[3]
    scale = HDIM ** (-0.5)

    def copy(src, dst, sems, to):
        return pltpu.make_async_remote_copy(
            src_ref=src,
            dst_ref=dst,
            send_sem=sems.at[0],
            recv_sem=sems.at[1],
            device_id=to,
            device_id_type=pl.DeviceIdType.MESH,
        )

    loads = [
        pltpu.make_async_copy(w_out_hbm, w_out_ref, w_sem.at[0]),
        pltpu.make_async_copy(w_qkv_hbm, w_qkv_ref, w_sem.at[1]),
        pltpu.make_async_copy(w_o_hbm, w_o_ref, w_sem.at[2]),
    ]
    for one in loads:
        one.start()

    barrier = pltpu.get_barrier_semaphore()
    greeted = [by_core, by_x, by_y] + [along(o) for o in range(1, n_mp)]
    for other in greeted:
        pl.semaphore_signal(
            barrier, inc=1, device_id=other, device_id_type=pl.DeviceIdType.MESH
        )
    pl.semaphore_wait(barrier, len(greeted))

    def block(o):
        return pl.ds(o * nodes, nodes)

    first, last = me == 0, me == n_mp - 1

    def relay(blocks, sems):
        def right(t):
            return copy(blocks.at[block(t)], blocks.at[block(t + 1)], sems.at[0, t], along(1))

        def left(t):
            return copy(
                blocks.at[block((n_mp - t) % n_mp)],
                blocks.at[block(n_mp - t - 1)],
                sems.at[1, t],
                along(-1),
            )

        def send(t):
            @pl.when(jnp.logical_and(me >= t, jnp.logical_not(last)))
            def _():
                right(t).start()

            @pl.when(jnp.logical_and(me + t <= n_mp - 1, jnp.logical_not(first)))
            def _():
                left(t).start()

        def hop(t, use=None):
            @pl.when(me >= t)
            def _():
                right(t - 1).wait_recv()

            @pl.when(me + t <= n_mp - 1)
            def _():
                left(t - 1).wait_recv()

            if t < n_mp - 1:
                send(t)
            if use is not None:

                @pl.when(me >= t)
                def _():
                    use(t)

                @pl.when(me + t <= n_mp - 1)
                def _():
                    use(n_mp - t)

        def drain():
            for t in range(n_mp - 1):

                @pl.when(jnp.logical_and(me >= t, jnp.logical_not(last)))
                def _(t=t):
                    right(t).wait_send()

                @pl.when(jnp.logical_and(me + t <= n_mp - 1, jnp.logical_not(first)))
                def _(t=t):
                    left(t).wait_send()

        return send, hop, drain

    cot_all[block(0), :] = cot_ref[...]
    cot_send, cot_hop, cot_drain = relay(cot_all, cot_sem)
    cot_send(0)

    row_ref[...] = jnp.zeros_like(row_ref)
    row_ref[0:1, :] = (source_ref[...] - me * grid_rows).astype(F32)
    row_ref[1:2, :] = (dest_ref[...] - (me - 1) * nodes).astype(F32)
    position = lax.broadcasted_iota(jnp.int32, (1, edges), 1)
    row_ref[2:3, :] = (position < count_ref[...]).astype(F32)
    row_ref[3 : 3 + attrs, :] = attr_ref[...]
    col_ref[...] = row_ref[...].T

    def project(j):
        at = span(j, 2 * TILE)
        value = nn(grid_ref[...], w_in_ref[:, at])
        high = value.astype(BF16)
        split_ref[pl.ds(0, grid_rows), at] = high
        split_ref[pl.ds(grid_rows, grid_rows), at] = (value - high.astype(F32)).astype(BF16)

    loop(c // (2 * TILE), project)

    source = col_ref[:, 0:1].astype(jnp.int32)
    place = lax.broadcasted_iota(jnp.int32, (edges, grid_rows), 1)
    table = (source == place).astype(F32).astype(BF16)
    table_ref[:, pl.ds(0, grid_rows)] = table
    table_ref[:, pl.ds(grid_rows, grid_rows)] = table

    def activate(j):
        at = span(j, TILE)
        pre = nn(table_ref[...], split_ref[:, at])
        for a in range(attrs):
            pre = pre + col_ref[:, 3 + a : 4 + a] * w_attr_ref[a : a + 1, at]
        sigma = 1.0 / (1.0 + jnp.exp(-pre))
        live = col_ref[:, 2:3]
        slope_ref[:, at] = sigma * (1.0 + pre * (1.0 - sigma)) * live
        hid_ref[:, at] = (pre * sigma * live).astype(BF16)

    loop(c // TILE, activate)
    cot_hop(1)
    loads[0].wait()

    def talk(j):
        at = span(j, TILE)
        msg_ref[:, at] = nn(hid_ref[...], w_out_ref[:, at]).astype(BF16)

    loop(c // TILE, talk)
    hops = min(2, n_mp - 1)
    if hops < n_mp - 1:
        cot_hop(hops)
        hops = hops + 1

    dest = dest_ref[...] - (me - 1) * nodes
    place = lax.broadcasted_iota(jnp.int32, (3 * nodes, edges), 0)
    dest_table = (dest == place).astype(F32).astype(BF16)

    def scatter(j):
        at = span(j, TILE)
        value = nn(dest_table_ref[...], msg_ref[:, at])
        hsend[0, :, at] = value[:nodes].astype(BF16)
        node_ref[:, at] = mesh_ref[:, at].astype(F32) + value[nodes : 2 * nodes]
        hsend[1, :, at] = value[2 * nodes :].astype(BF16)

    dest_table_ref[...] = dest_table
    loop(c // TILE, scatter)
    down = copy(hsend.at[0], hrecv.at[1], halo_sem.at[0], along(-1))
    up = copy(hsend.at[1], hrecv.at[0], halo_sem.at[1], along(1))

    def exchange(lower, upper, low_slot, high_slot):
        @pl.when(jnp.logical_not(first))
        def _():
            lower.start()

        @pl.when(jnp.logical_not(last))
        def _():
            upper.start()

        @pl.when(first)
        def _():
            low_slot[...] = jnp.zeros_like(low_slot)

        @pl.when(last)
        def _():
            high_slot[...] = jnp.zeros_like(high_slot)

    def settle(lower, upper):
        @pl.when(jnp.logical_not(first))
        def _():
            lower.wait_send()
            upper.wait_recv()

        @pl.when(jnp.logical_not(last))
        def _():
            upper.wait_send()
            lower.wait_recv()

    exchange(down, up, hrecv.at[0], hrecv.at[1])
    for t in range(hops, n_mp):
        cot_hop(t)
    settle(down, up)
    node = node_ref[...] + hrecv[0].astype(F32) + hrecv[1].astype(F32)
    inv = lax.rsqrt(jnp.mean(node * node, axis=-1, keepdims=True) + EPS)
    node_ref[...] = node
    x_all[block(0), :] = (node * inv).astype(BF16)

    x_send, x_hop, x_drain = relay(x_all, x_sem)
    x_send(0)

    def qkv(o):
        band = x_all[block(o), :]
        for i in range(3):
            qkvg[i, block(o), :] = nn(band, w_qkv_ref[i]).astype(BF16)

    loads[1].wait()
    qkv(0)
    cot_drain()
    loads[2].wait()
    qkvg[3] = nt(cot_all[...], w_o_ref[...]).astype(BF16)

    def turn(j):
        at = span(j, TILE)
        hid_t[at, :] = hid_ref[:, at].T
        grid_t[at, :] = grid_ref[:, at].T

    loop(c // TILE, turn)
    place = lax.broadcasted_iota(jnp.int32, (edges, 3 * nodes), 1)
    table = (col_ref[:, 1:2].astype(jnp.int32) == place).astype(F32) * col_ref[:, 2:3]
    gather_ref[...] = table.astype(BF16)
    place = lax.broadcasted_iota(jnp.int32, (grid_rows, edges), 0)
    source_table[...] = (source_ref[...] - me * grid_rows == place).astype(F32).astype(BF16)
    for t in range(1, n_mp):
        x_hop(t, qkv)
    x_drain()

    lane = lax.broadcasted_iota(jnp.int32, (1, LANES), 1)

    def heads(p):
        at = span(p, LANES)
        q, k, v, g = (qkvg[i, :, at] for i in range(4))
        sums = [0.0] * 4
        for h in range(LANES // HDIM):
            own = jnp.logical_and(lane >= h * HDIM, lane < (h + 1) * HDIM)
            own = own.astype(F32).astype(BF16)
            qh, kh, vh, gh = q * own, k * own, v * own, g * own
            scores = nt(kh, q) * scale
            probs = jnp.exp(scores - jnp.max(scores, axis=0, keepdims=True))
            probs = probs * (1.0 / jnp.sum(probs, axis=0, keepdims=True))
            probs_b = probs.astype(BF16)
            dprob = nt(vh, g)
            delta = jnp.sum(probs * dprob, axis=0, keepdims=True)
            dscore = (probs * (dprob - delta) * scale).astype(BF16)
            sums[0] = sums[0] + tn(kh, dscore)
            sums[1] = sums[1] + nn(dscore, qh)
            sums[2] = sums[2] + nn(probs_b, gh)
            sums[3] = sums[3] + tn(vh, probs_b)
        dqkv[0, :, at] = sums[0].T.astype(BF16)
        dqkv[1, :, at] = sums[1].astype(BF16)
        dqkv[2, :, at] = sums[2].astype(BF16)
        att_ref[:, at] = sums[3].T.astype(BF16)

    loop(width // LANES, heads)

    value = nt(dqkv[0], w_qkv_ref[0])
    value = value + nt(dqkv[1], w_qkv_ref[1])
    value = value + nt(dqkv[2], w_qkv_ref[2])
    dxs[...] = value.astype(BF16)

    def right_sum(k):
        return copy(dxs.at[block(n_mp - k)], dxr.at[0, k - 1], dx_sem.at[0, k - 1], along(1))

    def left_sum(k):
        return copy(dxs.at[block(k)], dxr.at[1, k - 1], dx_sem.at[1, k - 1], along(-1))

    def pass_on(k):
        def add_in(way, slot):
            held = dxs[block(slot), :].astype(F32) + dxr[way, k].astype(F32)
            dxs[block(slot), :] = held.astype(BF16)

        @pl.when(me + k <= n_mp - 1)
        def _():
            if k < n_mp - 1:

                @pl.when(jnp.logical_not(first))
                def _():
                    right_sum(k + 1).wait_recv()
                    add_in(0, n_mp - k)

            right_sum(k).start()

        @pl.when(me >= k)
        def _():
            if k < n_mp - 1:

                @pl.when(jnp.logical_not(last))
                def _():
                    left_sum(k + 1).wait_recv()
                    add_in(1, k)

            left_sum(k).start()

    def keep(j):
        return (j * 2 + px) * (1 - core) + (py * 2 + j) * core

    def give(j):
        return (j * 2 + 1 - px) * (1 - core) + ((1 - py) * 2 + j) * core

    def stage(group, number):
        sems = rs_sem.at[group]
        mine = parts.at[group]
        if number == 0:
            return [copy(mine.at[1 - core], r1.at[group], sems.at[0], by_core)]
        if number == 1:
            return [
                copy(mine.at[core, give(j)], r2.at[group, j], sems.at[1 + j], second)
                for j in range(2)
            ]
        rest = (1 - py) * (1 - core) + (1 - px) * core
        return [copy(mine.at[core, keep(rest)], r3.at[group], sems.at[3], third)]

    def begin(group, number):
        for one in stage(group, number):
            one.start()

    def add(group, slot, other):
        value = parts[group, core, slot].astype(F32) + other.astype(F32)
        parts[group, core, slot] = value.astype(BF16)

    def finish_first(group):
        for one in stage(group, 0):
            one.wait()
        for j in range(2):
            add(group, give(j), r1[group, give(j)])
        begin(group, 1)
        for j in range(2):
            add(group, keep(j), r1[group, keep(j)])

    def finish_second(group):
        for one in stage(group, 1):
            one.wait()
        rest = (1 - py) * (1 - core) + (1 - px) * core
        add(group, keep(rest), r2[group, rest])
        begin(group, 2)
        add(group, keep(1 - rest), r2[group, 1 - rest])

    def finish_third(group):
        for one in stage(group, 2):
            one.wait()
        return parts[group, core, py * 2 + px].astype(F32) + r3[group].astype(F32)

    def put(group, j, value, start=0):
        value = value.astype(BF16)
        for side in range(2):
            parts[group, side, j, :, start : start + value.shape[1]] = value[
                side * rows : (side + 1) * rows
            ]

    def pairs(group, fill):
        loop(parts.shape[2], fill)
        begin(group, 0)

    def fill_qk(j):
        x_part = x_all[:, span(j, 2 * rows)]
        for i in range(2):
            put(0, j, tn(x_part, dqkv[i]), i * width)

    def fill_vo(j):
        at = span(j, 2 * rows)
        put(1, j, tn(x_all[:, at], dqkv[2]))
        put(1, j, tn(cot_all[:, at], att_ref[...]), width)

    fills = [functools.partial(pairs, 0, fill_qk), functools.partial(pairs, 1, fill_vo)]
    for k in range(n_mp - 1, 0, -1):
        pass_on(k)
        if fills:
            fills.pop(0)()
    for fill in fills:
        fill()
    finish_first(0)

    for k in range(1, n_mp):

        @pl.when(me + k <= n_mp - 1)
        def _(k=k):
            right_sum(k).wait_send()

        @pl.when(me >= k)
        def _(k=k):
            left_sum(k).wait_send()

    @pl.when(first)
    def _():
        dxr[0, 0] = jnp.zeros_like(dxr[0, 0])

    @pl.when(last)
    def _():
        dxr[1, 0] = jnp.zeros_like(dxr[1, 0])

    @pl.when(jnp.logical_not(first))
    def _():
        right_sum(1).wait_recv()

    @pl.when(jnp.logical_not(last))
    def _():
        left_sum(1).wait_recv()

    dx = dxs[block(0), :].astype(F32) + dxr[0, 0].astype(F32) + dxr[1, 0].astype(F32)
    node = node_ref[...]
    inv = lax.rsqrt(jnp.mean(node * node, axis=-1, keepdims=True) + EPS)
    mean = jnp.mean(dx * node, axis=-1, keepdims=True)
    dnode = cot_ref[...].astype(F32) + inv * dx - node * inv * inv * inv * mean
    beside[pl.ds(nodes, nodes), :] = dnode.astype(BF16)
    middle = beside.at[pl.ds(nodes, nodes)]
    low, high = beside.at[pl.ds(0, nodes)], beside.at[pl.ds(2 * nodes, nodes)]
    down = copy(middle, high, beside_sem.at[0], along(-1))
    up = copy(middle, low, beside_sem.at[1], along(1))
    exchange(down, up, low, high)
    d_mesh_ref[...] = dnode.astype(BF16)
    finish_first(1)
    settle(down, up)

    def edge_gather(j):
        at = span(j, TILE)
        msg_ref[:, at] = nn(gather_ref[...], beside[:, at]).astype(BF16)

    loop(c // TILE, edge_gather)

    half = cols // 2

    def pieces(h):
        return [pl.ds(t * cols + h * half, half) for t in range(n_mp)]

    def spill(group, left, right_of):
        for u in range(0, n_mp, 2):
            value = nn(left[...], right_of(u)).astype(BF16)
            for r in range(2 * parts.shape[2]):
                parts[group, r % 2, r // 2, :, u * half : (u + 2) * half] = value[
                    r * rows : (r + 1) * rows
                ]
        begin(group, 0)

    def pair_of(ref, at, h, u):
        return jnp.concatenate([ref[at, piece] for piece in pieces(h)[u : u + 2]], axis=1)

    def grad_out(h):
        spill(2 + h, hid_t, lambda u: pair_of(msg_ref, pl.ds(0, edges), h, u))

    grad_out(0)
    finish_second(0)
    grad_out(1)
    finish_second(1)
    finish_first(2)

    def grad_in(h):
        for u in range(0, n_mp, 2):
            spots = pieces(h)[u : u + 2]
            weight = jnp.concatenate([w_out_ref[piece, :] for piece in spots], axis=0)
            dpre = nt(msg_ref[...], weight) * pair_of(slope_ref, pl.ds(0, edges), h, u)
            for a in range(attrs):
                value = jnp.sum(col_ref[:, 3 + a : 4 + a] * dpre, axis=0, keepdims=True)
                for t, piece in enumerate(spots):
                    at_own[a : a + 1, piece] = value[:, t * half : (t + 1) * half]
            dpre_ref[:, u * half : (u + 2) * half] = dpre.astype(BF16)
        dproj = nn(source_table[...], dpre_ref[...]).astype(BF16)
        for t, piece in enumerate(pieces(h)):
            dproj_ref[:, piece] = dproj[:, t * half : (t + 1) * half]
        spill(4 + h, grid_t, lambda u: pair_of(dproj_ref, pl.ds(0, grid_rows), h, u))

    grad_in(0)
    finish_first(3)
    finish_second(2)
    grad_in(1)
    finish_first(4)
    finish_second(3)

    attr_steps = [
        copy(at_own, at_recv.at[i], at_sem.at[i], to) for i, to in enumerate((by_core, by_x, by_y))
    ]
    attr_steps[0].start()

    def grid_back(j):
        at = span(j, 2 * TILE)
        d_grid_ref[:, at] = nt(dproj_ref[...], w_in_ref[at, :]).astype(BF16)

    finish_first(5)
    loop(c // (2 * TILE), grid_back)
    attr_steps[0].wait()
    at_own[...] = at_own[...] + at_recv[0]
    attr_steps[1].start()
    value = finish_third(0)
    for i in range(2):
        d_qkv_ref[i] = value[:, i * width : (i + 1) * width]
    value = finish_third(1)
    d_qkv_ref[2] = value[:, :width]
    d_o_ref[...] = value[:, width:].T

    def spread(group):
        slot = group - 2
        value = finish_third(group)
        for t in range(n_mp):
            mpb[slot, t] = value[:, t * half : (t + 1) * half].astype(BF16)
        copies = [
            copy(mpb.at[slot, (me + o) % n_mp], mpr.at[slot, o - 1], mp_sem.at[slot, o - 1], along(o))
            for o in range(1, n_mp)
        ]
        for one in copies:
            one.start()
        return copies

    def collect(group, copies, out_ref, h):
        slot = group - 2
        for one in copies:
            one.wait()
        value = mpb[slot, me].astype(F32)
        for o in range(1, n_mp):
            value = value + mpr[slot, o - 1].astype(F32)
        out_ref[:, h * half : (h + 1) * half] = value

    copies = [spread(2)]
    finish_second(4)
    copies.append(spread(3))
    attr_steps[1].wait()
    at_own[...] = at_own[...] + at_recv[1]
    attr_steps[2].start()
    finish_second(5)
    copies.append(spread(4))
    attr_steps[2].wait()
    at_all[0] = at_own[...] + at_recv[2]
    attr_copies = [
        copy(at_all.at[0], at_all.at[o], at_sem.at[2 + o], along(o)) for o in range(1, n_mp)
    ]
    for one in attr_copies:
        one.start()
    copies.append(spread(5))
    collect(2, copies[0], d_out_ref, 0)
    collect(3, copies[1], d_out_ref, 1)
    for one in attr_copies:
        one.wait()
    value = at_all[me]
    for s in range(1, n_mp):
        value = value + at_all[(me + n_mp - s) % n_mp]
    d_attr_ref[...] = value
    collect(4, copies[2], d_in_ref, 0)
    collect(5, copies[3], d_in_ref, 1)


def write_out(*refs):
    sems = refs[-1]
    count = len(refs) // 2
    copies = [
        pltpu.make_async_copy(refs[i], refs[count + i], sems.at[i]) for i in range(count)
    ]
    for one in copies:
        one.start()
    for one in copies:
        one.wait()


def fused(
    grid_latent,
    mesh_latent,
    edge_source,
    edge_dest,
    edge_count,
    edge_attr,
    w_attr,
    w_in,
    w_out,
    w_qkv,
    w_o,
    cotangent,
):
    n_dp, n_mp = lax.axis_size("dp"), lax.axis_size("mp")
    grid_rows, c = grid_latent.shape[1:]
    nodes = mesh_latent.shape[1]
    edges = edge_source.shape[1]
    attrs = w_attr.shape[0]
    width = w_qkv.shape[2]
    total = nodes * n_mp
    rows, cols = c // n_dp, c // n_mp
    vmem = pl.BlockSpec(memory_space=pltpu.VMEM)
    anywhere = pl.BlockSpec(memory_space=pl.ANY)
    shape = jax.ShapeDtypeStruct
    dma = pltpu.SemaphoreType.DMA
    outs = pl.pallas_call(
        functools.partial(layer_kernel, n_mp),
        out_shape=(
            shape((grid_rows, c), BF16),
            shape((nodes, c), BF16),
            shape((attrs, c), F32),
            shape((rows, cols), F32),
            shape((rows, cols), F32),
            shape((3, rows, width), F32),
            shape((width, rows), F32),
        ),
        in_specs=[vmem] * 8 + [anywhere] * 3 + [vmem],
        out_specs=[vmem] * 7,
        scratch_shapes=[
            pltpu.VMEM(w_out.shape, BF16),
            pltpu.VMEM(w_qkv.shape, BF16),
            pltpu.VMEM(w_o.shape, BF16),
            pltpu.VMEM((2 * grid_rows, c), BF16),
            pltpu.VMEM((edges, c), F32),
            pltpu.VMEM((edges, c), BF16),
            pltpu.VMEM((c, edges), BF16),
            pltpu.VMEM((c, grid_rows), BF16),
            pltpu.VMEM((edges, c), BF16),
            pltpu.VMEM(((attrs + 10) // 8 * 8, edges), F32),
            pltpu.VMEM((edges, (attrs + 10) // 8 * 8), F32),
            pltpu.VMEM((2, nodes, c), BF16),
            pltpu.VMEM((2, nodes, c), BF16),
            pltpu.VMEM((nodes, c), F32),
            pltpu.VMEM((total, c), BF16),
            pltpu.VMEM((total, c), BF16),
            pltpu.VMEM((4, total, width), BF16),
            pltpu.VMEM((3, total, width), BF16),
            pltpu.VMEM((total, width), BF16),
            pltpu.VMEM((total, c), BF16),
            pltpu.VMEM((2, n_mp - 1, nodes, c), BF16),
            pltpu.VMEM((3 * nodes, c), BF16),
            pltpu.VMEM((grid_rows, c), BF16),
            pltpu.VMEM((6, 2, n_dp // 2, rows, c // 2), BF16),
            pltpu.VMEM((6, n_dp // 2, rows, c // 2), BF16),
            pltpu.VMEM((6, 2, rows, c // 2), BF16),
            pltpu.VMEM((6, rows, c // 2), BF16),
            pltpu.VMEM((4, n_mp, rows, cols // 2), BF16),
            pltpu.VMEM((4, n_mp - 1, rows, cols // 2), BF16),
            pltpu.VMEM((edges, c // 2), BF16),
            pltpu.VMEM((edges, 2 * grid_rows), BF16),
            pltpu.VMEM((3 * nodes, edges), BF16),
            pltpu.VMEM((edges, 3 * nodes), BF16),
            pltpu.VMEM((grid_rows, edges), BF16),
            pltpu.VMEM((attrs, c), F32),
            pltpu.VMEM((3, attrs, c), F32),
            pltpu.VMEM((n_mp, attrs, c), F32),
            dma((2, n_mp - 1, 2)),
            dma((2, n_mp - 1, 2)),
            dma((2, 2)),
            dma((2, n_mp - 1, 2)),
            dma((2, 2)),
            dma((6, 4, 2)),
            dma((4, n_mp - 1, 2)),
            dma((2 + n_mp, 2)),
            dma((3,)),
        ],
        compiler_params=pltpu.CompilerParams(
            collective_id=0, has_side_effects=True, vmem_limit_bytes=58 * 2**20
        ),
    )(
        grid_latent[0],
        mesh_latent[0],
        edge_source,
        edge_dest,
        edge_count,
        edge_attr[0],
        w_attr,
        w_in,
        w_out,
        w_qkv,
        w_o,
        cotangent[0],
    )
    outs = pl.pallas_call(
        write_out,
        out_shape=tuple(shape(one.shape, one.dtype) for one in outs),
        in_specs=[vmem] * len(outs),
        out_specs=[anywhere] * len(outs),
        scratch_shapes=[dma((len(outs),))],
    )(*outs)
    return (outs[0][None], outs[1][None]) + tuple(outs[2:])


def step(*arrays):
    grid_latent, mesh_latent, edge_source, w_qkv = (arrays[i] for i in (0, 1, 2, 9))
    c, width = w_qkv.shape[1:]
    n_dp, n_mp = lax.axis_size("dp"), lax.axis_size("mp")
    fits = (
        n_dp == 8
        and n_mp % 2 == 0
        and n_mp * mesh_latent.shape[1] <= 512
        and 4 * width == c
        and width % (2 * LANES) == 0
        and c % (2 * TILE) == 0
        and (c // n_dp) % LANES == 0
        and edge_source.shape[1] % TILE == 0
        and grid_latent.shape[1] % LANES == 0
    )
    return fused(*arrays) if fits else shards(*arrays)


def solution(mesh):
    return jax.shard_map(
        step,
        mesh=mesh,
        in_specs=(
            P("dp", "mp", None),
            P("dp", "mp", None),
            P("dp", "mp"),
            P("dp", "mp"),
            P("dp", "mp"),
            P("dp", None, "mp"),
            P(),
            P(),
            P(),
            P(None, None, "mp"),
            P("mp", None),
            P("dp", "mp", None),
        ),
        out_specs=(
            P("dp", "mp", None),
            P("dp", "mp", None),
            P(),
            P("dp", "mp"),
            P("dp", "mp"),
            P(None, "dp", "mp"),
            P("mp", "dp"),
        ),
        check_vma=False,
    )
```

```python
import functools

import jax
import jax.numpy as jnp
from jax import lax
from jax.experimental import pallas as pl
from jax.experimental.pallas import tpu as pltpu
from jax.sharding import PartitionSpec as P

HDIM = 64


EPS = 1e-06


def shifted(block, axis, distance):
    devices = range(lax.axis_size(axis))
    route = [(i - distance, i) for i in devices if i - distance in devices]
    return lax.ppermute(block, axis, route)


def with_halo(block, sides, width):
    for axis, dim in sides:
        count = lax.axis_size(axis)
        forward = [(i, i + 1) for i in range(count - 1)]
        backward = [(target, source) for source, target in forward]
        low = lax.ppermute(
            lax.slice_in_dim(block, block.shape[dim] - width, None, axis=dim), axis, forward
        )
        high = lax.ppermute(lax.slice_in_dim(block, 0, width, axis=dim), axis, backward)
        block = jnp.concatenate([low, block, high], axis=dim)
    return block


def shards(
    grid_latent,
    mesh_latent,
    edge_source,
    edge_dest,
    edge_count,
    edge_attr,
    w_attr,
    w_in,
    w_out,
    w_qkv,
    w_o,
    cotangent,
):
    band = lax.axis_index("mp")
    grid_rows = grid_latent.shape[1]
    nodes = mesh_latent.shape[1]
    edges = edge_source.shape[1]
    grid = grid_latent[0]
    live = (jnp.arange(edges, dtype=jnp.int32) < edge_count[0, 0]).astype(jnp.float32)[:, None]
    source_local = edge_source[0] - band * grid_rows
    dest_local = edge_dest[0] - (band - 1) * nodes
    projected = jnp.dot(grid, w_in, preferred_element_type=jnp.float32)
    attr_terms = lax.dot_general(
        edge_attr[0],
        w_attr,
        (((0,), (0,)), ((), ())),
        precision=lax.Precision.HIGHEST,
        preferred_element_type=jnp.float32,
    )
    preact = projected[source_local] + attr_terms
    hidden = (jax.nn.silu(preact) * live).astype(jnp.bfloat16)
    message = jnp.dot(hidden, w_out, preferred_element_type=jnp.float32).astype(jnp.bfloat16)
    dest_table = (dest_local[:, None] == jnp.arange(3 * nodes, dtype=jnp.int32)[None, :]).astype(
        jnp.bfloat16
    )
    partial_rows = lax.dot_general(
        dest_table, message, (((0,), (0,)), ((), ())), preferred_element_type=jnp.float32
    )
    from_below = shifted(partial_rows[2 * nodes :], "mp", 1)
    from_above = shifted(partial_rows[:nodes], "mp", -1)
    node = (
        mesh_latent[0].astype(jnp.float32)
        + partial_rows[nodes : 2 * nodes]
        + from_below
        + from_above
    )
    inv = lax.rsqrt(jnp.mean(node * node, axis=-1, keepdims=True) + EPS)
    normed = (node * inv).astype(jnp.bfloat16)
    all_normed, all_cot = (
        lax.all_gather(normed, "mp", axis=0, tiled=True),
        lax.all_gather(cotangent[0], "mp", axis=0, tiled=True),
    )
    total = all_normed.shape[0]
    width = w_qkv.shape[2]
    local_heads = width // HDIM
    qkv = jnp.einsum("nc,icd->ind", all_normed, w_qkv, preferred_element_type=jnp.float32).astype(
        jnp.bfloat16
    )
    qkv = qkv.reshape(3, total, local_heads, HDIM)
    query, keys, values = (qkv[0], qkv[1], qkv[2])
    d_att = lax.dot_general(
        all_cot, w_o, (((1,), (1,)), ((), ())), preferred_element_type=jnp.float32
    ).astype(jnp.bfloat16)
    d_att = d_att.reshape(total, local_heads, HDIM)
    block = min(512, total)
    scale = HDIM ** (-0.5)

    def attend_block(carry, index):
        key_acc, value_acc = carry
        start = index * block
        query_blk = lax.dynamic_slice_in_dim(query, start, block, 0)
        grad_blk = lax.dynamic_slice_in_dim(d_att, start, block, 0)
        scores = (
            jnp.einsum("qhd,khd->hqk", query_blk, keys, preferred_element_type=jnp.float32) * scale
        )
        probs = jax.nn.softmax(scores, axis=-1)
        probs_b = probs.astype(jnp.bfloat16)
        attended = jnp.einsum(
            "hqk,khd->qhd", probs_b, values, preferred_element_type=jnp.float32
        ).astype(jnp.bfloat16)
        dprob = jnp.einsum("qhd,khd->hqk", grad_blk, values, preferred_element_type=jnp.float32)
        delta = jnp.sum(probs * dprob, axis=-1, keepdims=True)
        dscore = (probs * (dprob - delta) * scale).astype(jnp.bfloat16)
        dquery = jnp.einsum(
            "hqk,khd->qhd", dscore, keys, preferred_element_type=jnp.float32
        ).astype(jnp.bfloat16)
        key_acc = key_acc + jnp.einsum(
            "hqk,qhd->khd", dscore, query_blk, preferred_element_type=jnp.float32
        )
        value_acc = value_acc + jnp.einsum(
            "hqk,qhd->khd", probs_b, grad_blk, preferred_element_type=jnp.float32
        )
        return ((key_acc, value_acc), (attended, dquery))

    empty = jnp.zeros((total, local_heads, HDIM), jnp.float32)
    sums, blocks = lax.scan(
        attend_block, (empty, empty), jnp.arange(total // block, dtype=jnp.int32)
    )
    attended = blocks[0].reshape(total, width)
    dquery = blocks[1].reshape(total, width)
    dkeys = sums[0].astype(jnp.bfloat16).reshape(total, width)
    dvalues = sums[1].astype(jnp.bfloat16).reshape(total, width)
    dqkv = jnp.stack([dquery, dkeys, dvalues])
    dw_o = lax.dot_general(
        attended, all_cot, (((0,), (0,)), ((), ())), preferred_element_type=jnp.float32
    )
    dw_qkv = jnp.einsum("nc,ind->icd", all_normed, dqkv, preferred_element_type=jnp.float32)
    sum_qkv, sum_o = (
        lax.psum_scatter(dw_qkv.astype(jnp.bfloat16), "dp", scatter_dimension=1, tiled=True).astype(
            jnp.float32
        ),
        lax.psum_scatter(dw_o.astype(jnp.bfloat16), "dp", scatter_dimension=1, tiled=True).astype(
            jnp.float32
        ),
    )
    dx = lax.psum_scatter(
        jnp.einsum("ind,icd->nc", dqkv, w_qkv, preferred_element_type=jnp.float32).astype(
            jnp.bfloat16
        ),
        "mp",
        scatter_dimension=0,
        tiled=True,
    ).astype(jnp.float32)
    dnode = (
        cotangent[0].astype(jnp.float32)
        + inv * dx
        - node * inv * inv * inv * jnp.mean(dx * node, axis=-1, keepdims=True)
    )
    d_mesh = dnode.astype(jnp.bfloat16)
    beside_all = with_halo(d_mesh, (("mp", 0),), nodes)
    dmessage = (beside_all[dest_local].astype(jnp.float32) * live).astype(jnp.bfloat16)
    dw_out = lax.dot_general(
        hidden, dmessage, (((0,), (0,)), ((), ())), preferred_element_type=jnp.float32
    )
    dhidden = lax.dot_general(
        dmessage, w_out, (((1,), (1,)), ((), ())), preferred_element_type=jnp.float32
    )
    sigma = jax.nn.sigmoid(preact)
    dpre = dhidden * sigma * (1.0 + preact * (1.0 - sigma)) * live
    dw_attr = jnp.dot(
        edge_attr[0], dpre, precision=lax.Precision.HIGHEST, preferred_element_type=jnp.float32
    )
    source_table = (
        source_local[:, None] == jnp.arange(grid_rows, dtype=jnp.int32)[None, :]
    ).astype(jnp.bfloat16)
    dproj = lax.dot_general(
        source_table,
        dpre.astype(jnp.bfloat16),
        (((0,), (0,)), ((), ())),
        preferred_element_type=jnp.float32,
    ).astype(jnp.bfloat16)
    dw_in = lax.dot_general(
        grid, dproj, (((0,), (0,)), ((), ())), preferred_element_type=jnp.float32
    )
    d_grid = lax.dot_general(
        dproj, w_in, (((1,), (1,)), ((), ())), preferred_element_type=jnp.float32
    ).astype(jnp.bfloat16)
    sum_attr = lax.psum(dw_attr, ("dp", "mp"))
    first_in, first_out = (
        lax.psum_scatter(dw_in.astype(jnp.bfloat16), "dp", scatter_dimension=0, tiled=True).astype(
            jnp.float32
        ),
        lax.psum_scatter(dw_out.astype(jnp.bfloat16), "dp", scatter_dimension=0, tiled=True).astype(
            jnp.float32
        ),
    )
    sum_in, sum_out = (
        lax.psum_scatter(
            first_in.astype(jnp.bfloat16), "mp", scatter_dimension=1, tiled=True
        ).astype(jnp.float32),
        lax.psum_scatter(
            first_out.astype(jnp.bfloat16), "mp", scatter_dimension=1, tiled=True
        ).astype(jnp.float32),
    )
    return (d_grid[None], d_mesh[None], sum_attr, sum_in, sum_out, sum_qkv, sum_o)


F32 = jnp.float32
BF16 = jnp.bfloat16
LANES = 128
TILE = 256


def nn(a, b):
    return jnp.dot(a, b, preferred_element_type=F32)


def nt(a, b):
    return lax.dot_general(a, b, (((1,), (1,)), ((), ())), preferred_element_type=F32)


def tn(a, b):
    return lax.dot_general(a, b, (((0,), (0,)), ((), ())), preferred_element_type=F32)


def span(index, size):
    return pl.ds(pl.multiple_of(index * size, size), size)


def loop(count, body):
    def step(i, carry):
        body(i)
        return carry

    lax.fori_loop(0, count, step, 0)


def layer_kernel(
    n_mp,
    grid_ref,
    mesh_ref,
    source_ref,
    dest_ref,
    count_ref,
    attr_ref,
    w_attr_ref,
    w_in_ref,
    w_out_hbm,
    w_qkv_hbm,
    w_o_hbm,
    cot_ref,
    d_grid_ref,
    d_mesh_ref,
    d_attr_ref,
    d_in_ref,
    d_out_ref,
    d_qkv_ref,
    d_o_ref,
    w_out_ref,
    w_qkv_ref,
    w_o_ref,
    split_ref,
    slope_ref,
    hid_ref,
    hid_t,
    grid_t,
    msg_ref,
    row_ref,
    col_ref,
    hsend,
    hrecv,
    node_ref,
    x_all,
    cot_all,
    qkvg,
    dqkv,
    att_ref,
    dxs,
    dxr,
    beside,
    dproj_ref,
    parts,
    r1,
    r2,
    r3,
    mpb,
    mpr,
    dpre_ref,
    table_ref,
    dest_table_ref,
    gather_ref,
    source_table,
    at_own,
    at_recv,
    at_all,
    cot_sem,
    x_sem,
    halo_sem,
    dx_sem,
    beside_sem,
    rs_sem,
    mp_sem,
    at_sem,
    w_sem,
):
    d = lax.axis_index("dp")
    me = lax.axis_index("mp")
    core = d % 2
    px = (d // 2) % 2
    py = d // 4
    by_core = (d + 1 - 2 * core, me)
    by_x = (d + 2 - 4 * px, me)
    by_y = (d + 4 - 8 * py, me)
    second = (by_x[0] * (1 - core) + by_y[0] * core, me)
    third = (by_y[0] * (1 - core) + by_x[0] * core, me)

    def along(offset):
        return (d, (me + offset + n_mp) % n_mp)

    grid_rows, c = grid_ref.shape
    nodes = mesh_ref.shape[0]
    edges = source_ref.shape[1]
    attrs = w_attr_ref.shape[0]
    width = w_o_ref.shape[0]
    total = nodes * n_mp
    rows = parts.shape[3]
    cols = 2 * mpb.shape[3]
    scale = HDIM ** (-0.5)

    def copy(src, dst, sems, to):
        return pltpu.make_async_remote_copy(
            src_ref=src,
            dst_ref=dst,
            send_sem=sems.at[0],
            recv_sem=sems.at[1],
            device_id=to,
            device_id_type=pl.DeviceIdType.MESH,
        )

    loads = [
        pltpu.make_async_copy(w_out_hbm, w_out_ref, w_sem.at[0]),
        pltpu.make_async_copy(w_qkv_hbm, w_qkv_ref, w_sem.at[1]),
        pltpu.make_async_copy(w_o_hbm, w_o_ref, w_sem.at[2]),
    ]
    for one in loads:
        one.start()

    barrier = pltpu.get_barrier_semaphore()
    greeted = [by_core, by_x, by_y] + [along(o) for o in range(1, n_mp)]
    for other in greeted:
        pl.semaphore_signal(
            barrier, inc=1, device_id=other, device_id_type=pl.DeviceIdType.MESH
        )
    pl.semaphore_wait(barrier, len(greeted))

    def block(o):
        return pl.ds(o * nodes, nodes)

    first, last = me == 0, me == n_mp - 1

    def relay(blocks, sems):
        def right(t):
            return copy(blocks.at[block(t)], blocks.at[block(t + 1)], sems.at[0, t], along(1))

        def left(t):
            return copy(
                blocks.at[block((n_mp - t) % n_mp)],
                blocks.at[block(n_mp - t - 1)],
                sems.at[1, t],
                along(-1),
            )

        def send(t):
            @pl.when(jnp.logical_and(me >= t, jnp.logical_not(last)))
            def _():
                right(t).start()

            @pl.when(jnp.logical_and(me + t <= n_mp - 1, jnp.logical_not(first)))
            def _():
                left(t).start()

        def hop(t, use=None):
            @pl.when(me >= t)
            def _():
                right(t - 1).wait_recv()

            @pl.when(me + t <= n_mp - 1)
            def _():
                left(t - 1).wait_recv()

            if t < n_mp - 1:
                send(t)
            if use is not None:

                @pl.when(me >= t)
                def _():
                    use(t)

                @pl.when(me + t <= n_mp - 1)
                def _():
                    use(n_mp - t)

        def drain():
            for t in range(n_mp - 1):

                @pl.when(jnp.logical_and(me >= t, jnp.logical_not(last)))
                def _(t=t):
                    right(t).wait_send()

                @pl.when(jnp.logical_and(me + t <= n_mp - 1, jnp.logical_not(first)))
                def _(t=t):
                    left(t).wait_send()

        return send, hop, drain

    cot_all[block(0), :] = cot_ref[...]
    cot_send, cot_hop, cot_drain = relay(cot_all, cot_sem)
    cot_send(0)

    row_ref[...] = jnp.zeros_like(row_ref)
    row_ref[0:1, :] = (source_ref[...] - me * grid_rows).astype(F32)
    row_ref[1:2, :] = (dest_ref[...] - (me - 1) * nodes).astype(F32)
    position = lax.broadcasted_iota(jnp.int32, (1, edges), 1)
    row_ref[2:3, :] = (position < count_ref[...]).astype(F32)
    row_ref[3 : 3 + attrs, :] = attr_ref[...]
    col_ref[...] = row_ref[...].T

    def project(j):
        at = span(j, 2 * TILE)
        value = nn(grid_ref[...], w_in_ref[:, at])
        high = value.astype(BF16)
        split_ref[pl.ds(0, grid_rows), at] = high
        split_ref[pl.ds(grid_rows, grid_rows), at] = (value - high.astype(F32)).astype(BF16)

    loop(c // (2 * TILE), project)

    source = col_ref[:, 0:1].astype(jnp.int32)
    place = lax.broadcasted_iota(jnp.int32, (edges, grid_rows), 1)
    table = (source == place).astype(F32).astype(BF16)
    table_ref[:, pl.ds(0, grid_rows)] = table
    table_ref[:, pl.ds(grid_rows, grid_rows)] = table

    def activate(j):
        at = span(j, TILE)
        pre = nn(table_ref[...], split_ref[:, at])
        for a in range(attrs):
            pre = pre + col_ref[:, 3 + a : 4 + a] * w_attr_ref[a : a + 1, at]
        sigma = 1.0 / (1.0 + jnp.exp(-pre))
        live = col_ref[:, 2:3]
        slope_ref[:, at] = sigma * (1.0 + pre * (1.0 - sigma)) * live
        hid_ref[:, at] = (pre * sigma * live).astype(BF16)

    loop(c // TILE, activate)
    cot_hop(1)
    loads[0].wait()

    def talk(j):
        at = span(j, TILE)
        msg_ref[:, at] = nn(hid_ref[...], w_out_ref[:, at]).astype(BF16)

    loop(c // TILE, talk)

    dest = dest_ref[...] - (me - 1) * nodes
    place = lax.broadcasted_iota(jnp.int32, (3 * nodes, edges), 0)
    dest_table = (dest == place).astype(F32).astype(BF16)

    def scatter(j):
        at = span(j, TILE)
        value = nn(dest_table_ref[...], msg_ref[:, at])
        hsend[0, :, at] = value[:nodes].astype(BF16)
        node_ref[:, at] = mesh_ref[:, at].astype(F32) + value[nodes : 2 * nodes]
        hsend[1, :, at] = value[2 * nodes :].astype(BF16)

    dest_table_ref[...] = dest_table
    loop(c // TILE, scatter)
    down = copy(hsend.at[0], hrecv.at[1], halo_sem.at[0], along(-1))
    up = copy(hsend.at[1], hrecv.at[0], halo_sem.at[1], along(1))

    def exchange(lower, upper, low_slot, high_slot):
        @pl.when(jnp.logical_not(first))
        def _():
            lower.start()

        @pl.when(jnp.logical_not(last))
        def _():
            upper.start()

        @pl.when(first)
        def _():
            low_slot[...] = jnp.zeros_like(low_slot)

        @pl.when(last)
        def _():
            high_slot[...] = jnp.zeros_like(high_slot)

    def settle(lower, upper):
        @pl.when(jnp.logical_not(first))
        def _():
            lower.wait_send()
            upper.wait_recv()

        @pl.when(jnp.logical_not(last))
        def _():
            upper.wait_send()
            lower.wait_recv()

    exchange(down, up, hrecv.at[0], hrecv.at[1])
    for t in range(2, n_mp - 1):
        cot_hop(t)
    settle(down, up)
    node = node_ref[...] + hrecv[0].astype(F32) + hrecv[1].astype(F32)
    inv = lax.rsqrt(jnp.mean(node * node, axis=-1, keepdims=True) + EPS)
    node_ref[...] = node
    x_all[block(0), :] = (node * inv).astype(BF16)

    x_send, x_hop, x_drain = relay(x_all, x_sem)
    x_send(0)

    def qkv(o):
        band = x_all[block(o), :]
        for i in range(3):
            qkvg[i, block(o), :] = nn(band, w_qkv_ref[i]).astype(BF16)

    loads[1].wait()
    qkv(0)
    if n_mp > 2:
        cot_hop(n_mp - 1)
    cot_drain()
    loads[2].wait()
    qkvg[3] = nt(cot_all[...], w_o_ref[...]).astype(BF16)

    def turn(j):
        at = span(j, TILE)
        hid_t[at, :] = hid_ref[:, at].T
        grid_t[at, :] = grid_ref[:, at].T

    loop(c // TILE, turn)
    place = lax.broadcasted_iota(jnp.int32, (edges, 3 * nodes), 1)
    table = (col_ref[:, 1:2].astype(jnp.int32) == place).astype(F32) * col_ref[:, 2:3]
    gather_ref[...] = table.astype(BF16)
    place = lax.broadcasted_iota(jnp.int32, (grid_rows, edges), 0)
    source_table[...] = (source_ref[...] - me * grid_rows == place).astype(F32).astype(BF16)
    for t in range(1, n_mp):
        x_hop(t, qkv)
    x_drain()

    lane = lax.broadcasted_iota(jnp.int32, (1, LANES), 1)

    def heads(p):
        at = span(p, LANES)
        q, k, v, g = (qkvg[i, :, at] for i in range(4))
        sums = [0.0] * 4
        for h in range(LANES // HDIM):
            own = jnp.logical_and(lane >= h * HDIM, lane < (h + 1) * HDIM)
            own = own.astype(F32).astype(BF16)
            qh, kh, vh, gh = q * own, k * own, v * own, g * own
            scores = nt(kh, q) * scale
            probs = jnp.exp(scores - jnp.max(scores, axis=0, keepdims=True))
            probs = probs * (1.0 / jnp.sum(probs, axis=0, keepdims=True))
            probs_b = probs.astype(BF16)
            dprob = nt(vh, g)
            delta = jnp.sum(probs * dprob, axis=0, keepdims=True)
            dscore = (probs * (dprob - delta) * scale).astype(BF16)
            sums[0] = sums[0] + tn(kh, dscore)
            sums[1] = sums[1] + nn(dscore, qh)
            sums[2] = sums[2] + nn(probs_b, gh)
            sums[3] = sums[3] + tn(vh, probs_b)
        dqkv[0, :, at] = sums[0].T.astype(BF16)
        dqkv[1, :, at] = sums[1].astype(BF16)
        dqkv[2, :, at] = sums[2].astype(BF16)
        att_ref[:, at] = sums[3].T.astype(BF16)

    loop(width // LANES, heads)

    value = nt(dqkv[0], w_qkv_ref[0])
    value = value + nt(dqkv[1], w_qkv_ref[1])
    value = value + nt(dqkv[2], w_qkv_ref[2])
    dxs[...] = value.astype(BF16)

    def right_sum(k):
        return copy(dxs.at[block(n_mp - k)], dxr.at[0, k - 1], dx_sem.at[0, k - 1], along(1))

    def left_sum(k):
        return copy(dxs.at[block(k)], dxr.at[1, k - 1], dx_sem.at[1, k - 1], along(-1))

    def pass_on(k):
        def add_in(way, slot):
            held = dxs[block(slot), :].astype(F32) + dxr[way, k].astype(F32)
            dxs[block(slot), :] = held.astype(BF16)

        @pl.when(me + k <= n_mp - 1)
        def _():
            if k < n_mp - 1:

                @pl.when(jnp.logical_not(first))
                def _():
                    right_sum(k + 1).wait_recv()
                    add_in(0, n_mp - k)

            right_sum(k).start()

        @pl.when(me >= k)
        def _():
            if k < n_mp - 1:

                @pl.when(jnp.logical_not(last))
                def _():
                    left_sum(k + 1).wait_recv()
                    add_in(1, k)

            left_sum(k).start()

    def keep(j):
        return (j * 2 + px) * (1 - core) + (py * 2 + j) * core

    def give(j):
        return (j * 2 + 1 - px) * (1 - core) + ((1 - py) * 2 + j) * core

    def stage(group, number):
        sems = rs_sem.at[group]
        mine = parts.at[group]
        if number == 0:
            return [copy(mine.at[1 - core], r1.at[group], sems.at[0], by_core)]
        if number == 1:
            return [
                copy(mine.at[core, give(j)], r2.at[group, j], sems.at[1 + j], second)
                for j in range(2)
            ]
        rest = (1 - py) * (1 - core) + (1 - px) * core
        return [copy(mine.at[core, keep(rest)], r3.at[group], sems.at[3], third)]

    def begin(group, number):
        for one in stage(group, number):
            one.start()

    def add(group, slot, other):
        value = parts[group, core, slot].astype(F32) + other.astype(F32)
        parts[group, core, slot] = value.astype(BF16)

    def finish_first(group):
        for one in stage(group, 0):
            one.wait()
        for j in range(2):
            add(group, give(j), r1[group, give(j)])
        begin(group, 1)
        for j in range(2):
            add(group, keep(j), r1[group, keep(j)])

    def finish_second(group):
        for one in stage(group, 1):
            one.wait()
        rest = (1 - py) * (1 - core) + (1 - px) * core
        add(group, keep(rest), r2[group, rest])
        begin(group, 2)
        add(group, keep(1 - rest), r2[group, 1 - rest])

    def finish_third(group):
        for one in stage(group, 2):
            one.wait()
        return parts[group, core, py * 2 + px].astype(F32) + r3[group].astype(F32)

    def put(group, j, value, start=0):
        value = value.astype(BF16)
        for side in range(2):
            parts[group, side, j, :, start : start + value.shape[1]] = value[
                side * rows : (side + 1) * rows
            ]

    def pairs(group, fill):
        loop(parts.shape[2], fill)
        begin(group, 0)

    def fill_qk(j):
        x_part = x_all[:, span(j, 2 * rows)]
        for i in range(2):
            put(0, j, tn(x_part, dqkv[i]), i * width)

    def fill_vo(j):
        at = span(j, 2 * rows)
        put(1, j, tn(x_all[:, at], dqkv[2]))
        put(1, j, tn(cot_all[:, at], att_ref[...]), width)

    fills = [functools.partial(pairs, 0, fill_qk), functools.partial(pairs, 1, fill_vo)]
    for k in range(n_mp - 1, 0, -1):
        pass_on(k)
        if fills:
            fills.pop(0)()
    for fill in fills:
        fill()
    finish_first(0)

    for k in range(1, n_mp):

        @pl.when(me + k <= n_mp - 1)
        def _(k=k):
            right_sum(k).wait_send()

        @pl.when(me >= k)
        def _(k=k):
            left_sum(k).wait_send()

    @pl.when(first)
    def _():
        dxr[0, 0] = jnp.zeros_like(dxr[0, 0])

    @pl.when(last)
    def _():
        dxr[1, 0] = jnp.zeros_like(dxr[1, 0])

    @pl.when(jnp.logical_not(first))
    def _():
        right_sum(1).wait_recv()

    @pl.when(jnp.logical_not(last))
    def _():
        left_sum(1).wait_recv()

    dx = dxs[block(0), :].astype(F32) + dxr[0, 0].astype(F32) + dxr[1, 0].astype(F32)
    node = node_ref[...]
    inv = lax.rsqrt(jnp.mean(node * node, axis=-1, keepdims=True) + EPS)
    mean = jnp.mean(dx * node, axis=-1, keepdims=True)
    dnode = cot_ref[...].astype(F32) + inv * dx - node * inv * inv * inv * mean
    beside[pl.ds(nodes, nodes), :] = dnode.astype(BF16)
    middle = beside.at[pl.ds(nodes, nodes)]
    low, high = beside.at[pl.ds(0, nodes)], beside.at[pl.ds(2 * nodes, nodes)]
    down = copy(middle, high, beside_sem.at[0], along(-1))
    up = copy(middle, low, beside_sem.at[1], along(1))
    exchange(down, up, low, high)
    d_mesh_ref[...] = dnode.astype(BF16)
    finish_first(1)
    settle(down, up)

    def edge_gather(j):
        at = span(j, TILE)
        msg_ref[:, at] = nn(gather_ref[...], beside[:, at]).astype(BF16)

    loop(c // TILE, edge_gather)

    half = cols // 2

    def pieces(h):
        return [pl.ds(t * cols + h * half, half) for t in range(n_mp)]

    def spill(group, left, right_of):
        for u in range(0, n_mp, 2):
            value = nn(left[...], right_of(u)).astype(BF16)
            for r in range(2 * parts.shape[2]):
                parts[group, r % 2, r // 2, :, u * half : (u + 2) * half] = value[
                    r * rows : (r + 1) * rows
                ]
        begin(group, 0)

    def pair_of(ref, at, h, u):
        return jnp.concatenate([ref[at, piece] for piece in pieces(h)[u : u + 2]], axis=1)

    def grad_out(h):
        spill(2 + h, hid_t, lambda u: pair_of(msg_ref, pl.ds(0, edges), h, u))

    grad_out(0)
    finish_second(0)
    grad_out(1)
    finish_second(1)
    finish_first(2)

    def grad_in(h):
        for u in range(0, n_mp, 2):
            spots = pieces(h)[u : u + 2]
            weight = jnp.concatenate([w_out_ref[piece, :] for piece in spots], axis=0)
            dpre = nt(msg_ref[...], weight) * pair_of(slope_ref, pl.ds(0, edges), h, u)
            for a in range(attrs):
                value = jnp.sum(col_ref[:, 3 + a : 4 + a] * dpre, axis=0, keepdims=True)
                for t, piece in enumerate(spots):
                    at_own[a : a + 1, piece] = value[:, t * half : (t + 1) * half]
            dpre_ref[:, u * half : (u + 2) * half] = dpre.astype(BF16)
        dproj = nn(source_table[...], dpre_ref[...]).astype(BF16)
        for t, piece in enumerate(pieces(h)):
            dproj_ref[:, piece] = dproj[:, t * half : (t + 1) * half]
        spill(4 + h, grid_t, lambda u: pair_of(dproj_ref, pl.ds(0, grid_rows), h, u))

    grad_in(0)
    finish_first(3)
    finish_second(2)
    grad_in(1)
    finish_first(4)
    finish_second(3)

    attr_steps = [
        copy(at_own, at_recv.at[i], at_sem.at[i], to) for i, to in enumerate((by_core, by_x, by_y))
    ]
    attr_steps[0].start()

    def grid_back(j):
        at = span(j, 2 * TILE)
        d_grid_ref[:, at] = nt(dproj_ref[...], w_in_ref[at, :]).astype(BF16)

    finish_first(5)
    loop(c // (2 * TILE), grid_back)
    attr_steps[0].wait()
    at_own[...] = at_own[...] + at_recv[0]
    attr_steps[1].start()
    value = finish_third(0)
    for i in range(2):
        d_qkv_ref[i] = value[:, i * width : (i + 1) * width]
    value = finish_third(1)
    d_qkv_ref[2] = value[:, :width]
    d_o_ref[...] = value[:, width:].T

    def spread(group):
        slot = group - 2
        value = finish_third(group)
        for t in range(n_mp):
            mpb[slot, t] = value[:, t * half : (t + 1) * half].astype(BF16)
        copies = [
            copy(mpb.at[slot, (me + o) % n_mp], mpr.at[slot, o - 1], mp_sem.at[slot, o - 1], along(o))
            for o in range(1, n_mp)
        ]
        for one in copies:
            one.start()
        return copies

    def collect(group, copies, out_ref, h):
        slot = group - 2
        for one in copies:
            one.wait()
        value = mpb[slot, me].astype(F32)
        for o in range(1, n_mp):
            value = value + mpr[slot, o - 1].astype(F32)
        out_ref[:, h * half : (h + 1) * half] = value

    copies = [spread(2)]
    finish_second(4)
    copies.append(spread(3))
    attr_steps[1].wait()
    at_own[...] = at_own[...] + at_recv[1]
    attr_steps[2].start()
    finish_second(5)
    copies.append(spread(4))
    attr_steps[2].wait()
    at_all[0] = at_own[...] + at_recv[2]
    attr_copies = [
        copy(at_all.at[0], at_all.at[o], at_sem.at[2 + o], along(o)) for o in range(1, n_mp)
    ]
    for one in attr_copies:
        one.start()
    copies.append(spread(5))
    collect(2, copies[0], d_out_ref, 0)
    collect(3, copies[1], d_out_ref, 1)
    for one in attr_copies:
        one.wait()
    value = at_all[me]
    for s in range(1, n_mp):
        value = value + at_all[(me + n_mp - s) % n_mp]
    d_attr_ref[...] = value
    collect(4, copies[2], d_in_ref, 0)
    collect(5, copies[3], d_in_ref, 1)


def write_out(*refs):
    sems = refs[-1]
    count = len(refs) // 2
    copies = [
        pltpu.make_async_copy(refs[i], refs[count + i], sems.at[i]) for i in range(count)
    ]
    for one in copies:
        one.start()
    for one in copies:
        one.wait()


def fused(
    grid_latent,
    mesh_latent,
    edge_source,
    edge_dest,
    edge_count,
    edge_attr,
    w_attr,
    w_in,
    w_out,
    w_qkv,
    w_o,
    cotangent,
):
    n_dp, n_mp = lax.axis_size("dp"), lax.axis_size("mp")
    grid_rows, c = grid_latent.shape[1:]
    nodes = mesh_latent.shape[1]
    edges = edge_source.shape[1]
    attrs = w_attr.shape[0]
    width = w_qkv.shape[2]
    total = nodes * n_mp
    rows, cols = c // n_dp, c // n_mp
    vmem = pl.BlockSpec(memory_space=pltpu.VMEM)
    anywhere = pl.BlockSpec(memory_space=pl.ANY)
    shape = jax.ShapeDtypeStruct
    dma = pltpu.SemaphoreType.DMA
    outs = pl.pallas_call(
        functools.partial(layer_kernel, n_mp),
        out_shape=(
            shape((grid_rows, c), BF16),
            shape((nodes, c), BF16),
            shape((attrs, c), F32),
            shape((rows, cols), F32),
            shape((rows, cols), F32),
            shape((3, rows, width), F32),
            shape((width, rows), F32),
        ),
        in_specs=[vmem] * 8 + [anywhere] * 3 + [vmem],
        out_specs=[vmem] * 7,
        scratch_shapes=[
            pltpu.VMEM(w_out.shape, BF16),
            pltpu.VMEM(w_qkv.shape, BF16),
            pltpu.VMEM(w_o.shape, BF16),
            pltpu.VMEM((2 * grid_rows, c), BF16),
            pltpu.VMEM((edges, c), F32),
            pltpu.VMEM((edges, c), BF16),
            pltpu.VMEM((c, edges), BF16),
            pltpu.VMEM((c, grid_rows), BF16),
            pltpu.VMEM((edges, c), BF16),
            pltpu.VMEM(((attrs + 10) // 8 * 8, edges), F32),
            pltpu.VMEM((edges, (attrs + 10) // 8 * 8), F32),
            pltpu.VMEM((2, nodes, c), BF16),
            pltpu.VMEM((2, nodes, c), BF16),
            pltpu.VMEM((nodes, c), F32),
            pltpu.VMEM((total, c), BF16),
            pltpu.VMEM((total, c), BF16),
            pltpu.VMEM((4, total, width), BF16),
            pltpu.VMEM((3, total, width), BF16),
            pltpu.VMEM((total, width), BF16),
            pltpu.VMEM((total, c), BF16),
            pltpu.VMEM((2, n_mp - 1, nodes, c), BF16),
            pltpu.VMEM((3 * nodes, c), BF16),
            pltpu.VMEM((grid_rows, c), BF16),
            pltpu.VMEM((6, 2, n_dp // 2, rows, c // 2), BF16),
            pltpu.VMEM((6, n_dp // 2, rows, c // 2), BF16),
            pltpu.VMEM((6, 2, rows, c // 2), BF16),
            pltpu.VMEM((6, rows, c // 2), BF16),
            pltpu.VMEM((4, n_mp, rows, cols // 2), BF16),
            pltpu.VMEM((4, n_mp - 1, rows, cols // 2), BF16),
            pltpu.VMEM((edges, c // 2), BF16),
            pltpu.VMEM((edges, 2 * grid_rows), BF16),
            pltpu.VMEM((3 * nodes, edges), BF16),
            pltpu.VMEM((edges, 3 * nodes), BF16),
            pltpu.VMEM((grid_rows, edges), BF16),
            pltpu.VMEM((attrs, c), F32),
            pltpu.VMEM((3, attrs, c), F32),
            pltpu.VMEM((n_mp, attrs, c), F32),
            dma((2, n_mp - 1, 2)),
            dma((2, n_mp - 1, 2)),
            dma((2, 2)),
            dma((2, n_mp - 1, 2)),
            dma((2, 2)),
            dma((6, 4, 2)),
            dma((4, n_mp - 1, 2)),
            dma((2 + n_mp, 2)),
            dma((3,)),
        ],
        compiler_params=pltpu.CompilerParams(
            collective_id=0, has_side_effects=True, vmem_limit_bytes=58 * 2**20
        ),
    )(
        grid_latent[0],
        mesh_latent[0],
        edge_source,
        edge_dest,
        edge_count,
        edge_attr[0],
        w_attr,
        w_in,
        w_out,
        w_qkv,
        w_o,
        cotangent[0],
    )
    outs = pl.pallas_call(
        write_out,
        out_shape=tuple(shape(one.shape, one.dtype) for one in outs),
        in_specs=[vmem] * len(outs),
        out_specs=[anywhere] * len(outs),
        scratch_shapes=[dma((len(outs),))],
    )(*outs)
    return (outs[0][None], outs[1][None]) + tuple(outs[2:])


def step(*arrays):
    grid_latent, mesh_latent, edge_source, w_qkv = (arrays[i] for i in (0, 1, 2, 9))
    c, width = w_qkv.shape[1:]
    n_dp, n_mp = lax.axis_size("dp"), lax.axis_size("mp")
    fits = (
        n_dp == 8
        and n_mp % 2 == 0
        and n_mp * mesh_latent.shape[1] <= 512
        and 4 * width == c
        and width % (2 * LANES) == 0
        and c % (2 * TILE) == 0
        and (c // n_dp) % LANES == 0
        and edge_source.shape[1] % TILE == 0
        and grid_latent.shape[1] % LANES == 0
    )
    return fused(*arrays) if fits else shards(*arrays)


def solution(mesh):
    return jax.shard_map(
        step,
        mesh=mesh,
        in_specs=(
            P("dp", "mp", None),
            P("dp", "mp", None),
            P("dp", "mp"),
            P("dp", "mp"),
            P("dp", "mp"),
            P("dp", None, "mp"),
            P(),
            P(),
            P(),
            P(None, None, "mp"),
            P("mp", None),
            P("dp", "mp", None),
        ),
        out_specs=(
            P("dp", "mp", None),
            P("dp", "mp", None),
            P(),
            P("dp", "mp"),
            P("dp", "mp"),
            P(None, "dp", "mp"),
            P("mp", "dp"),
        ),
        check_vma=False,
    )
```
